128 devices in a mesh: dp: 16 (over z_lo, x, core), tensor: 8 (over y, z_hi).
Axes of the slice: x: 4, y: 4, z: 4 (z_hi: 2, z_lo: 2; z = z_hi * 2 + z_lo), core: 2. Of those that a mesh axis runs over, the one named last changes fastest.
Arguments:
- tokens: bfloat16 [1024, 8192], P('tensor', 'dp'), may hold values from -6 to 6
- segment_ids: int32 [1024], replicated, may hold values from 0 to 7, never falling along the last dimension, each value on 1 to 256 neighbouring positions
- gate_weight: bfloat16 [8192, 15360], P('dp', 'tensor'), may hold values from -0.0625 to 0.0625
- up_weight: bfloat16 [8192, 15360], P('dp', 'tensor'), may hold values from -0.0625 to 0.0625
- down_weight: bfloat16 [15360, 8192], P('tensor', 'dp'), may hold values from -0.046875 to 0.046875
- grad_out: bfloat16 [1024, 8192], P('tensor', 'dp'), may hold values from -6 to 6
Outputs:
- mixed: bfloat16 [1024, 8192], P('tensor', 'dp')
- grad_gate: float32 [8192, 15360], P('dp', 'tensor')
- grad_up: float32 [8192, 15360], P('dp', 'tensor')
- grad_down: float32 [15360, 8192], P('tensor', 'dp')
The draws below stay inside these ranges and needn't reach their ends.
Inputs may be any that keep to these rules, and one draw needn't show every extreme that they name: `segment_ids`: document numbers never fall along the positions; each of the 8 documents has 1 to 256 positions and one has exactly 256.
All inputs are finite; a program needn't handle non-finite values.
Results may differ from the reference program's by a relative error of at most 0.005.
Values may be sent and summed in bfloat16 or wider, within the bound.
A program may use at most 192 MiB of HBM per device.

```python
import math
import jax
import jax.numpy as jnp
import numpy as np
from jax import lax

D = 8192
FF = 15360
NSEG = 8
TOKENS = 1024
MOST = 256


def shard_levels(key, shape, cuts, low, top_value):
    def one(position, shards_of):
        draws = jax.random.uniform(jax.random.fold_in(jax.random.fold_in(key, 6), position), (shards_of,), jnp.float32, low / len(cuts), top_value / len(cuts))
        return jnp.repeat(jnp.exp(draws), shape[position] // shards_of).reshape((-1,) + (1,) * (len(shape) - position - 1))

    gain = one(*cuts[0])
    for cut in cuts[1:]:
        gain = gain * one(*cut)
    return gain


def length_profile(number_of, total, bound, lean):
    weights = [(1 << 20) // math.isqrt(rank ** lean) + 1 for rank in range(2, number_of + 1)]
    spare, given = total - bound - (number_of - 1), [1] * (number_of - 1)
    while spare > 0:
        free = [i for i in range(number_of - 1) if given[i] < bound]
        pool, left = sum([weights[i] for i in free]), spare
        for i in free:
            addition = min(bound - given[i], max(1, left * weights[i] // pool), spare)
            given[i] = given[i] + addition
            spare = spare - addition
    return np.array([bound] + given)


def uneven(rng, number_of, total, most, skew):
    if number_of == 2:
        one = jax.random.randint(rng, (), max(1, total - most), min(most, total - 1) + 1)
        return jnp.stack([one, total - one])
    tallies = jnp.asarray(length_profile(number_of, total, most, skew), jnp.int32)
    twos = (number_of - 1) // 2
    donor, sink = tallies[1:1 + 2 * twos:2], tallies[2:2 + 2 * twos:2]
    margin = jnp.minimum(donor - 1, most - sink)
    moved = jax.random.randint(jax.random.fold_in(rng, 1), (twos,), 0, 1 << 20) % (margin + 1)
    tallies = tallies.at[1:1 + 2 * twos:2].set(donor - moved).at[2:2 + 2 * twos:2].set(sink + moved)
    return tallies[jax.random.permutation(jax.random.fold_in(rng, 2), number_of)]


def normal_values(stream_key, dims, scale, most, pieces=(), kind=jnp.bfloat16):
    array = scale * jax.random.normal(stream_key, dims, jnp.float32)
    if pieces:
        array = array * shard_levels(stream_key, dims, pieces, -0.22, 0.18)
    return jnp.clip(array, -most, most).astype(kind)


def setup_inputs(seed: int = 0) -> dict:
    keys = jax.random.split(jax.random.key(seed), 7)
    return {
        "tokens": normal_values(keys[0], (TOKENS, D), 1.0, 6.0, ((0, 8), (1, 16))),
        "segment_ids": jnp.searchsorted(jnp.cumsum(uneven(keys[1], NSEG, TOKENS, MOST, 1)), jnp.arange(TOKENS), side="right").astype(jnp.int32),
        "gate_weight": normal_values(keys[2], (D, FF), D ** -0.5, 0.0625, ((0, 16), (1, 8))),
        "up_weight": normal_values(keys[3], (D, FF), D ** -0.5, 0.0625, ((0, 16), (1, 8))),
        "down_weight": normal_values(keys[4], (FF, D), FF ** -0.5, 0.046875, ((0, 8), (1, 16))),
        "grad_out": normal_values(keys[5], (TOKENS, D), 1.0, 6.0, ((0, 8), (1, 16))),
    }


def reference(tokens, segment_ids, gate_weight, up_weight, down_weight, grad_out):
    gate = jnp.dot(tokens, gate_weight, preferred_element_type=jnp.float32)
    up = jnp.dot(tokens, up_weight, preferred_element_type=jnp.float32)
    sig = jax.nn.sigmoid(gate)
    hidden = (gate * sig * up).astype(jnp.bfloat16)
    mixed = jnp.dot(hidden, down_weight, preferred_element_type=jnp.float32).astype(jnp.bfloat16)
    onehot = (segment_ids[:, None] == jnp.arange(NSEG, dtype=jnp.int32)[None, :]).astype(jnp.float32)
    lengths = lax.optimization_barrier(jnp.sum(onehot, axis=0))
    row_weight = lax.rsqrt(lax.optimization_barrier(jnp.sum(onehot * lengths[None, :], axis=1)))
    scaled = (grad_out.astype(jnp.float32) * row_weight[:, None]).astype(jnp.bfloat16)
    grad_down = jnp.dot(hidden.T, scaled, preferred_element_type=jnp.float32)
    dhidden = lax.dot_general(scaled, down_weight, (((1,), (1,)), ((), ())), preferred_element_type=jnp.float32)
    dgate = (dhidden * up * sig * (1.0 + gate * (1.0 - sig))).astype(jnp.bfloat16)
    dup = (dhidden * gate * sig).astype(jnp.bfloat16)
    grad_gate = jnp.dot(tokens.T, dgate, preferred_element_type=jnp.float32)
    grad_up = jnp.dot(tokens.T, dup, preferred_element_type=jnp.float32)
    return (mixed, grad_gate, grad_up, grad_down)
```

```python
import jax
import jax.numpy as jnp
from jax import lax
from jax.experimental import pallas as pl
from jax.experimental.pallas import tpu as pltpu
from jax.sharding import PartitionSpec as P

NSEG = 8
SLOTS = 8
ROWS = 128
HALF = 64
SEG = 16
WIDTH = 512
UNITS = 1920
TILE = 128
MESH = pl.DeviceIdType.MESH
BF16 = jnp.bfloat16
F32 = jnp.float32
DOT_COLUMNS = ((0, 512), (512, 512), (1024, 512), (1536, 384))

CA = 1152
CB = UNITS - CA
OA = -(-CA // (2 * TILE)) * TILE
KA = CA - OA
OB = -(-CB // (2 * TILE)) * TILE
KB = CB - OB
OL = OB // (2 * TILE) * TILE
OR = OB - OL

NAMES = (
    "core0", "core1", "core2", "x1p", "x1m", "x2p", "x2m", "zred", "zgat", "g1p", "g1m", "g2p", "g2m", "cgat",
    "mix", "y0", "y1p", "y1m", "y2p", "y2m", "k1p", "k1m", "k2p", "k2m", "k3",
)
KIND = {name: i for i, name in enumerate(NAMES)}


def exchange_kernel(
    ids_hbm, tokens_hbm, grad_out_hbm, wg_hbm, wu_hbm, wd_hbm,
    mown, gat, tokt, hidt, hh,
    ids, grad_out, wg, wu, wd, acc, cs, cr, x1s, x1a, x1b, x2s, x2r, zs, zr,
    y0s, y0r, y1s, y1a, y1b, y2s, y2r, ms, mr,
    ss, rs, ts, tr, ws, own_sems,
):
    inputs = [
        pltpu.make_async_copy(a, b, own_sems.at[k])
        for k, (a, b) in enumerate(
            ((ids_hbm, ids), (grad_out_hbm, grad_out), (tokens_hbm, gat.at[0, :, :WIDTH]))
        )
    ]
    for copy in inputs:
        copy.start()
    weights = [
        pltpu.make_async_copy(a, b, ws.at[k])
        for k, (a, b) in enumerate(((wg_hbm, wg), (wu_hbm, wu), (wd_hbm, wd)))
    ]
    for copy in weights:
        copy.start()

    dp = lax.axis_index("dp")
    tn = lax.axis_index("tensor")
    w, x, q = dp // 8, (dp // 2) % 4, dp % 2
    y, h = tn // 2, tn % 2
    xp, xm, xo = (x + 1) % 4, (x + 3) % 4, (x + 2) % 4

    def dpdev(w=w, x=x, q=q):
        return (w * 8 + x * 2 + q, tn)

    def tdev(dy, dh):
        return (dp, ((y + dy) % 4) * 2 + (h + dh) % 2)

    core, right, left, zmate = dpdev(q=1 - q), dpdev(x=xp), dpdev(x=xm), dpdev(w=1 - w)
    offsets = [(0, 0), (1, 0), (3, 0), (0, 1), (1, 1), (3, 1), (2, 1), (2, 0)]

    barrier = pltpu.get_barrier_semaphore()
    partners = [core, right, left, zmate] + [tdev(*o) for o in offsets[1:]]
    for p in partners:
        pl.semaphore_signal(barrier, inc=1, device_id=p, device_id_type=MESH)

    for copy in inputs:
        copy.wait()
    all_ids = ids[...]
    own_ids = ids[pl.ds(tn, 1), :]
    row = jnp.zeros((1, ROWS), F32)
    for s in range(NSEG):
        length = jnp.sum(jnp.where(all_ids == s, 1.0, 0.0), axis=(0, 1), keepdims=True)
        row = jnp.where(own_ids == s, lax.rsqrt(length), row)
    square = jnp.broadcast_to(row, (ROWS, ROWS))
    on_diagonal = lax.broadcasted_iota(jnp.int32, (ROWS, ROWS), 0) == lax.broadcasted_iota(
        jnp.int32, (ROWS, ROWS), 1
    )
    column = jnp.sum(jnp.where(on_diagonal, square, 0.0), axis=1, keepdims=True)
    gat[0, :, WIDTH:] = (grad_out[...].astype(F32) * column).astype(BF16)

    pl.semaphore_wait(barrier, len(partners))

    def rows_of(xx):
        return pl.ds(pl.multiple_of(q * HALF + xx * SEG, SEG), SEG)

    def seg_of(xx):
        return pl.ds(pl.multiple_of(xx * SEG, SEG), SEG)

    def half_of(qq):
        return pl.ds(pl.multiple_of(qq * HALF, HALF), HALF)

    def cols_of(start, size):
        return pl.ds(pl.multiple_of(start, TILE), size)

    def msg(name, c, src, dst, dev):
        kind = KIND[name]
        return pltpu.make_async_remote_copy(
            src_ref=src, dst_ref=dst, send_sem=ss.at[kind, c], recv_sem=rs.at[kind, c],
            device_id=dev, device_id_type=MESH,
        )

    def tok_msg(slot, src, dev):
        return pltpu.make_async_remote_copy(
            src_ref=src, dst_ref=gat.at[slot], send_sem=ts.at[slot], recv_sem=tr.at[slot],
            device_id=dev, device_id_type=MESH,
        )

    def in_place(name, c, rows, cols, dev):
        ref = hh.at[c, :, rows, cols]
        return msg(name, c, ref, ref, dev)

    own_a, mate_a = cols_of(w * KA, OA), cols_of((1 - w) * KA, OA)
    out_a, in_a = cols_of(w * OA, KA), cols_of((1 - w) * OA, KA)
    own_b, mate_b = cols_of(CA + w * KB, OB), cols_of(CA + (1 - w) * KB, OB)
    own_b_left = cols_of(CA + w * KB, OL)
    own_b_right = cols_of(CA + w * KB + OL, OR)
    out_b, in_b = cols_of(CA + w * OB, KB), cols_of(CA + (1 - w) * OB, KB)
    all_a, lo_a, hi_a = pl.ds(0, CA), pl.ds(0, OA), pl.ds(OA, KA)

    def m_core(c, k):
        return msg(f"core{k}", c, cs.at[c % 2, k], cr.at[c % 3, k], core)

    def m_x1p(c):
        return msg("x1p", c, x1s.at[c, :, :, lo_a], x1a.at[c], right)

    def m_x1m(c):
        return msg("x1m", c, x1s.at[c, :, :, hi_a], x1b.at[c], left)

    def m_x2p(c):
        return msg("x2p", c, x2s.at[c, 0], x2r.at[c, 0], right)

    def m_x2m(c):
        return msg("x2m", c, x2s.at[c, 1], x2r.at[c, 1], left)

    def m_zred(c):
        return msg("zred", c, zs.at[c], zr.at[c], zmate)

    def m_zgat(c, cols):
        return in_place("zgat", c, rows_of(x), cols, zmate)

    def m_g1p(c, xx):
        return in_place("g1p", c, rows_of(xx), all_a, right)

    def m_g1m(c, xx):
        return in_place("g1m", c, rows_of(xx), all_a, left)

    def m_g2p(c, xx):
        return in_place("g2p", c, rows_of(xx), hi_a, right)

    def m_g2m(c, xx):
        return in_place("g2m", c, rows_of(xx), lo_a, left)

    def m_y0(c):
        return msg("y0", c, y0s.at[c], y0r.at[c], zmate)

    def m_y1p(c):
        return msg("y1p", c, y1s.at[c, :, :, :OL], y1a.at[c], right)

    def m_y1m(c):
        return msg("y1m", c, y1s.at[c, :, :, OL:], y1b.at[c], left)

    def m_y2p(c):
        return msg("y2p", c, y2s.at[c, 0], y2r.at[c, 0], right)

    def m_y2m(c):
        return msg("y2m", c, y2s.at[c, 1], y2r.at[c, 1], left)

    def m_k1p(c, xx):
        return in_place("k1p", c, rows_of(xx), own_b, right)

    def m_k1m(c, xx):
        return in_place("k1m", c, rows_of(xx), own_b, left)

    def m_k2p(c, xx):
        return in_place("k2p", c, rows_of(xx), own_b_right, right)

    def m_k2m(c, xx):
        return in_place("k2m", c, rows_of(xx), own_b_left, left)

    def m_k3(c, cols):
        return in_place("k3", c, half_of(q), cols, zmate)

    def m_cgat(c, qq):
        ref = hh.at[c, :, half_of(qq), :]
        return msg("cgat", c, ref, ref, core)

    def m_mix(c):
        dy = jnp.where(c >= 6, 2, c % 3 + c % 3 // 2)
        return msg("mix", c, ms.at[c], mr.at[c], tdev(dy, (c + 1) // 4 % 2))

    for s in (1, 2, 3, 7):
        dy, dh = offsets[s]
        tok_msg(s, gat.at[0], tdev(-dy % 4, dh)).start()
    for copy in weights:
        copy.wait()

    def a_partials(c):
        @pl.when((c != 0) & (c != 3))
        def _():
            tok_msg(c, gat.at[0], core).wait_recv()

        both = jnp.concatenate([gat[c, half_of(1 - q), :], gat[c, half_of(q), :]], axis=0)
        tok, sc = both[:, :WIDTH], both[:, WIDTH:]
        for k, mat in enumerate((wg, wu, wd)):
            for n0, nw in DOT_COLUMNS:
                cols = slice(n0, n0 + nw)
                if k < 2:
                    part = jnp.dot(tok, mat[:, cols], preferred_element_type=F32)
                else:
                    part = lax.dot_general(
                        sc, mat[cols, :], (((1,), (1,)), ((), ())), preferred_element_type=F32
                    )
                cs[c % 2, k, :, cols] = part[:HALF]
                acc[c % 5, k, :, cols] = part[HALF:]
            m_core(c, k).start()

    def forward_tokens():
        tok_msg(3, gat.at[0], core).wait_recv()
        for s in (4, 5, 6):
            tok_msg(s, gat.at[3], tdev(-offsets[s][0] % 4, 0)).start()

    def b_stage(c):
        a = c % 5
        for k in range(3):
            m_core(c, k).wait_recv()
        acc[a] += cr[c % 3]
        x1s[c] = acc[a, :, seg_of(xo), :CA].astype(BF16)
        m_x1p(c).start()
        m_x1m(c).start()
        y0s[c] = acc[a, :, :, mate_b].astype(BF16)
        m_y0(c).start()
        for k in range(3):
            m_core(c, k).wait_send()

    def c_stage(c):
        a = c % 5
        m_x1p(c).wait_recv()
        m_x1m(c).wait_recv()
        acc[a, :, seg_of(xp), :OA] += x1a[c].astype(F32)
        acc[a, :, seg_of(xm), OA:CA] += x1b[c].astype(F32)
        x2s[c, 0] = acc[a, :, seg_of(xp), :CA].astype(BF16)
        x2s[c, 1] = acc[a, :, seg_of(xm), :CA].astype(BF16)
        m_x2p(c).start()
        m_x2m(c).start()

    def c2_stage(c):
        a = c % 5
        m_y0(c).wait_recv()
        acc[a, :, :, own_b] += y0r[c].astype(F32)
        y1s[c] = acc[a, :, seg_of(xo), own_b].astype(BF16)
        m_y1p(c).start()
        m_y1m(c).start()

    def d_stage(c):
        a = c % 5
        m_x2p(c).wait_recv()
        m_x2m(c).wait_recv()
        acc[a, :, seg_of(x), :CA] += x2r[c, 0].astype(F32) + x2r[c, 1].astype(F32)
        zs[c] = acc[a, :, seg_of(x), mate_a].astype(BF16)
        m_zred(c).start()

    def d2_stage(c):
        a = c % 5
        m_y1p(c).wait_recv()
        m_y1m(c).wait_recv()
        acc[a, :, seg_of(xp), own_b_left] += y1a[c].astype(F32)
        acc[a, :, seg_of(xm), own_b_right] += y1b[c].astype(F32)
        y2s[c, 0] = acc[a, :, seg_of(xp), own_b].astype(BF16)
        y2s[c, 1] = acc[a, :, seg_of(xm), own_b].astype(BF16)
        m_y2p(c).start()
        m_y2m(c).start()

    def finish_units(c, tot, cols):
        gate, up, dhid = tot[0], tot[1], tot[2]
        sig = jax.nn.sigmoid(gate)
        hh[c, 0, rows_of(x), cols] = (gate * sig * up).astype(BF16)
        hh[c, 1, rows_of(x), cols] = (dhid * up * sig * (1.0 + gate * (1.0 - sig))).astype(BF16)
        hh[c, 2, rows_of(x), cols] = (dhid * gate * sig).astype(BF16)

    def e_stage(c):
        a = c % 5
        m_zred(c).wait_recv()
        finish_units(c, acc[a, :, seg_of(x), own_a] + zr[c].astype(F32), own_a)
        m_zgat(c, out_a).start()

    def e2_stage(c):
        a = c % 5
        m_y2p(c).wait_recv()
        m_y2m(c).wait_recv()
        tot = acc[a, :, seg_of(x), own_b] + y2r[c, 0].astype(F32) + y2r[c, 1].astype(F32)
        finish_units(c, tot, own_b)
        m_k1p(c, x).start()
        m_k1m(c, x).start()

    def f_stage(c):
        m_zgat(c, in_a).wait_recv()
        m_g1p(c, x).start()
        m_g1m(c, x).start()

    def f2_stage(c):
        m_k1p(c, xm).wait_recv()
        m_k2p(c, xm).start()
        m_k1m(c, xp).wait_recv()
        m_k2m(c, xp).start()

    def g_stage(c):
        m_g1p(c, xm).wait_recv()
        m_g2p(c, xm).start()
        m_g1m(c, xp).wait_recv()
        m_g2m(c, xp).start()

    def g2_stage(c):
        m_k2p(c, xo).wait_recv()
        m_k2m(c, xo).wait_recv()
        m_k3(c, out_b).start()

    def h_stage(c):
        m_g2p(c, xo).wait_recv()
        m_g2m(c, xo).wait_recv()
        m_k3(c, in_b).wait_recv()
        m_cgat(c, q).start()

    def i_stage(c):
        m_cgat(c, 1 - q).wait_recv()
        part = jnp.dot(hh[c, 0], wd[...], preferred_element_type=F32)

        @pl.when(c == 0)
        def _():
            mown[...] = part

        @pl.when(c != 0)
        def _():
            ms[c] = part.astype(BF16)
            m_mix(c).start()

        tokens_c = cols_of(c * ROWS, ROWS)
        hidt[:, tokens_c] = hh[c, 0].T
        tokt[:, tokens_c] = gat[c, :, :WIDTH].T

    plan = [
        (e_stage, 5, False), (c_stage, 2, False), (g2_stage, 8, True), (g_stage, 11, True),
        (f_stage, 9, True), (b_stage, 1, False), (d_stage, 3, False), (f2_stage, 6, True),
        (a_partials, 0, False), (h_stage, 12, True), (e2_stage, 4, False), (c2_stage, 2, False),
        (d2_stage, 3, False), (i_stage, 13, True),
    ]
    last = max(lag for _, lag, _ in plan)

    def step(i, carry):
        for stage, lag, back in plan:
            j = i - lag
            c = (j + 1) % SLOTS if back else j

            @pl.when((j >= 0) & (j < SLOTS))
            def _(stage=stage, c=c):
                stage(c)

        @pl.when(i == 2)
        def _():
            forward_tokens()

        return carry

    lax.fori_loop(0, SLOTS + last, step, 0)

    def finish(c, carry):
        m_mix(c).wait_recv()
        mown[...] += mr[c].astype(F32)
        return carry

    lax.fori_loop(1, SLOTS, finish, 0)

    def drain(c, carry):
        for message in (
            m_x1p(c), m_x1m(c), m_x2p(c), m_x2m(c), m_zred(c), m_zgat(c, out_a),
            m_g1p(c, x), m_g1m(c, x), m_g2p(c, xm), m_g2m(c, xp), m_cgat(c, q),
            m_y0(c), m_y1p(c), m_y1m(c), m_y2p(c), m_y2m(c), m_k1p(c, x), m_k1m(c, x),
            m_k2p(c, xm), m_k2m(c, xp), m_k3(c, out_b),
        ):
            message.wait_send()

        @pl.when(c != 0)
        def _():
            m_mix(c).wait_send()
            tok_msg(c, gat.at[0], core).wait_send()

        return carry

    lax.fori_loop(0, SLOTS, drain, 0)


def exchange(ids, tokens, grad_out, wg, wu, wd):
    vmem = pl.BlockSpec(memory_space=pltpu.VMEM)
    hbm = pl.BlockSpec(memory_space=pltpu.HBM)
    total = SLOTS * ROWS
    kinds = len(NAMES)
    return pl.pallas_call(
        exchange_kernel,
        name="exchange",
        out_shape=(
            pltpu.VMEM((ROWS, WIDTH), F32),
            pltpu.VMEM((SLOTS, ROWS, 2 * WIDTH), BF16),
            pltpu.VMEM((WIDTH, total), BF16),
            pltpu.VMEM((UNITS, total), BF16),
            pltpu.VMEM((SLOTS, 3, ROWS, UNITS), BF16),
        ),
        in_specs=[hbm] * 6,
        out_specs=(vmem,) * 5,
        scratch_shapes=[
            pltpu.VMEM((SLOTS, ROWS), jnp.int32),
            pltpu.VMEM((ROWS, WIDTH), BF16),
            pltpu.VMEM((WIDTH, UNITS), BF16),
            pltpu.VMEM((WIDTH, UNITS), BF16),
            pltpu.VMEM((UNITS, WIDTH), BF16),
            pltpu.VMEM((5, 3, HALF, UNITS), F32),
            pltpu.VMEM((2, 3, HALF, UNITS), F32),
            pltpu.VMEM((3, 3, HALF, UNITS), F32),
            pltpu.VMEM((SLOTS, 3, SEG, CA), BF16),
            pltpu.VMEM((SLOTS, 3, SEG, OA), BF16),
            pltpu.VMEM((SLOTS, 3, SEG, KA), BF16),
            pltpu.VMEM((SLOTS, 2, 3, SEG, CA), BF16),
            pltpu.VMEM((SLOTS, 2, 3, SEG, CA), BF16),
            pltpu.VMEM((SLOTS, 3, SEG, OA), BF16),
            pltpu.VMEM((SLOTS, 3, SEG, OA), BF16),
            pltpu.VMEM((SLOTS, 3, HALF, OB), BF16),
            pltpu.VMEM((SLOTS, 3, HALF, OB), BF16),
            pltpu.VMEM((SLOTS, 3, SEG, OB), BF16),
            pltpu.VMEM((SLOTS, 3, SEG, OL), BF16),
            pltpu.VMEM((SLOTS, 3, SEG, OR), BF16),
            pltpu.VMEM((SLOTS, 2, 3, SEG, OB), BF16),
            pltpu.VMEM((SLOTS, 2, 3, SEG, OB), BF16),
            pltpu.VMEM((SLOTS, ROWS, WIDTH), BF16),
            pltpu.VMEM((SLOTS, ROWS, WIDTH), BF16),
            pltpu.SemaphoreType.DMA((kinds, SLOTS)),
            pltpu.SemaphoreType.DMA((kinds, SLOTS)),
            pltpu.SemaphoreType.DMA((SLOTS,)),
            pltpu.SemaphoreType.DMA((SLOTS,)),
            pltpu.SemaphoreType.DMA((3,)),
            pltpu.SemaphoreType.DMA((3,)),
        ],
        compiler_params=pltpu.CompilerParams(
            collective_id=0, has_side_effects=True, vmem_limit_bytes=35 * 2**20
        ),
        cost_estimate=pl.CostEstimate(
            flops=8 * total * WIDTH * UNITS, bytes_accessed=24 * 2**20, transcendentals=0
        ),
    )(ids, tokens, grad_out, wg, wu, wd)


GRAD_COLUMNS = 640


def grads_kernel(
    mown, gat, tokt, hidt, hh, mixed, grad_gate, grad_up, grad_down,
    mbuf, gbuf, ubuf, dbuf, sems, msem,
):
    total = SLOTS * ROWS
    mbuf[...] = mown[...].astype(BF16)
    mcopy = pltpu.make_async_copy(mbuf, mixed, msem)
    mcopy.start()
    tok_t = tokt[...]
    sc = gat[:, :, WIDTH:].reshape(total, WIDTH)
    blocks = []
    for n in range(UNITS // GRAD_COLUMNS):
        cols = pl.ds(n * GRAD_COLUMNS, GRAD_COLUMNS)
        slot = n % 2
        copies = [
            pltpu.make_async_copy(gbuf.at[slot], grad_gate.at[:, cols], sems.at[0, slot]),
            pltpu.make_async_copy(ubuf.at[slot], grad_up.at[:, cols], sems.at[1, slot]),
            pltpu.make_async_copy(dbuf.at[slot], grad_down.at[cols, :], sems.at[2, slot]),
        ]
        blocks.append(copies)
        for k, buf in enumerate((gbuf, ubuf, dbuf)):
            if n >= 2:
                blocks[n - 2][k].wait()
            if k < 2:
                right = hh[:, k + 1, :, cols].reshape(total, GRAD_COLUMNS)
                buf[slot] = jnp.dot(tok_t, right, preferred_element_type=F32)
            else:
                buf[slot] = jnp.dot(hidt[cols, :], sc, preferred_element_type=F32)
            copies[k].start()
    for copies in blocks[-2:]:
        for copy in copies:
            copy.wait()
    mcopy.wait()


def grads(mown, gat, tokt, hidt, hh):
    total = SLOTS * ROWS
    vmem = pl.BlockSpec(memory_space=pltpu.VMEM)
    hbm = pl.BlockSpec(memory_space=pl.ANY)
    return pl.pallas_call(
        grads_kernel,
        name="grads",
        out_shape=(
            jax.ShapeDtypeStruct((ROWS, WIDTH), BF16),
            jax.ShapeDtypeStruct((WIDTH, UNITS), F32),
            jax.ShapeDtypeStruct((WIDTH, UNITS), F32),
            jax.ShapeDtypeStruct((UNITS, WIDTH), F32),
        ),
        in_specs=[vmem] * 5,
        out_specs=(hbm,) * 4,
        scratch_shapes=[
            pltpu.VMEM((ROWS, WIDTH), BF16),
            pltpu.VMEM((2, WIDTH, GRAD_COLUMNS), F32),
            pltpu.VMEM((2, WIDTH, GRAD_COLUMNS), F32),
            pltpu.VMEM((2, GRAD_COLUMNS, WIDTH), F32),
            pltpu.SemaphoreType.DMA((3, 2)),
            pltpu.SemaphoreType.DMA,
        ],
        compiler_params=pltpu.CompilerParams(vmem_limit_bytes=32 * 2**20),
        cost_estimate=pl.CostEstimate(
            flops=6 * total * WIDTH * UNITS, bytes_accessed=12 * 2**20, transcendentals=0
        ),
    )(mown, gat, tokt, hidt, hh)


def shards(tokens, segment_ids, gate_weight, up_weight, down_weight, grad_out):
    ids = segment_ids.reshape(SLOTS, ROWS)
    outs = exchange(ids, tokens, grad_out, gate_weight, up_weight, down_weight)
    return grads(*outs)


def solution(mesh):
    placed = (
        P("tensor", "dp"),
        P(),
        P("dp", "tensor"),
        P("dp", "tensor"),
        P("tensor", "dp"),
        P("tensor", "dp"),
    )
    return jax.shard_map(
        shards,
        mesh=mesh,
        in_specs=placed,
        out_specs=(P("tensor", "dp"), P("dp", "tensor"), P("dp", "tensor"), P("tensor", "dp")),
        check_vma=False,
    )
```

```python
import jax
import jax.numpy as jnp
from jax import lax
from jax.experimental import pallas as pl
from jax.experimental.pallas import tpu as pltpu
from jax.sharding import PartitionSpec as P

NSEG = 8
SLOTS = 8
ROWS = 128
HALF = 64
SEG = 16
WIDTH = 512
UNITS = 1920
TILE = 128
MESH = pl.DeviceIdType.MESH
BF16 = jnp.bfloat16
F32 = jnp.float32
DOT_COLUMNS = ((0, 512), (512, 512), (1024, 512), (1536, 384))

JOIN = 19

CA = 1152
CB = UNITS - CA
OA = -(-CA // (2 * TILE)) * TILE
KA = CA - OA
OB = -(-CB // (2 * TILE)) * TILE
KB = CB - OB
OL = OB // (2 * TILE) * TILE
OR = OB - OL

NAMES = (
    "core0", "core1", "core2", "x1p", "x1m", "x2p", "x2m", "zred", "zgat", "g1p", "g1m", "g2p", "g2m", "cgat",
    "mix", "y0", "y1p", "y1m", "y2p", "y2m", "k1p", "k1m", "k2p", "k2m", "k3",
)
KIND = {name: i for i, name in enumerate(NAMES)}


def exchange_kernel(
    ids_hbm, tokens_hbm, grad_out_hbm, wg_hbm, wu_hbm, wd_hbm,
    mown, gat, tokt, hidt, hh,
    ids, grad_out, wg, wu, wd, acc, cs, cr, x1s, x1a, x1b, x2s, x2r, zs, zr,
    y0s, y0r, y1s, y1a, y1b, y2s, y2r, ms, mr, mfar,
    ss, rs, ts, tr, ws, own_sems,
):
    inputs = [
        pltpu.make_async_copy(a, b, own_sems.at[k])
        for k, (a, b) in enumerate(
            ((ids_hbm, ids), (grad_out_hbm, grad_out), (tokens_hbm, gat.at[0, :, :WIDTH]))
        )
    ]
    for copy in inputs:
        copy.start()
    weights = [
        pltpu.make_async_copy(a, b, ws.at[k])
        for k, (a, b) in enumerate(((wg_hbm, wg), (wu_hbm, wu), (wd_hbm, wd)))
    ]
    for copy in weights:
        copy.start()

    dp = lax.axis_index("dp")
    tn = lax.axis_index("tensor")
    w, x, q = dp // 8, (dp // 2) % 4, dp % 2
    y, h = tn // 2, tn % 2
    xp, xm, xo = (x + 1) % 4, (x + 3) % 4, (x + 2) % 4

    def dpdev(w=w, x=x, q=q):
        return (w * 8 + x * 2 + q, tn)

    def tdev(dy, dh):
        return (dp, ((y + dy) % 4) * 2 + (h + dh) % 2)

    core, right, left, zmate = dpdev(q=1 - q), dpdev(x=xp), dpdev(x=xm), dpdev(w=1 - w)
    offsets = [(0, 0), (1, 0), (3, 0), (0, 1), (1, 1), (3, 1), (2, 1), (2, 0)]

    barrier = pltpu.get_barrier_semaphore()
    partners = [core, right, left, zmate] + [tdev(*o) for o in offsets[1:]]
    for p in partners:
        pl.semaphore_signal(barrier, inc=1, device_id=p, device_id_type=MESH)

    for copy in inputs:
        copy.wait()
    all_ids = ids[...]
    own_ids = ids[pl.ds(tn, 1), :]
    row = jnp.zeros((1, ROWS), F32)
    for s in range(NSEG):
        length = jnp.sum(jnp.where(all_ids == s, 1.0, 0.0), axis=(0, 1), keepdims=True)
        row = jnp.where(own_ids == s, lax.rsqrt(length), row)
    square = jnp.broadcast_to(row, (ROWS, ROWS))
    on_diagonal = lax.broadcasted_iota(jnp.int32, (ROWS, ROWS), 0) == lax.broadcasted_iota(
        jnp.int32, (ROWS, ROWS), 1
    )
    column = jnp.sum(jnp.where(on_diagonal, square, 0.0), axis=1, keepdims=True)
    gat[0, :, WIDTH:] = (grad_out[...].astype(F32) * column).astype(BF16)

    pl.semaphore_wait(barrier, len(partners))

    def rows_of(xx):
        return pl.ds(pl.multiple_of(q * HALF + xx * SEG, SEG), SEG)

    def seg_of(xx):
        return pl.ds(pl.multiple_of(xx * SEG, SEG), SEG)

    def half_of(qq):
        return pl.ds(pl.multiple_of(qq * HALF, HALF), HALF)

    def cols_of(start, size):
        return pl.ds(pl.multiple_of(start, TILE), size)

    def msg(name, c, src, dst, dev):
        kind = KIND[name]
        return pltpu.make_async_remote_copy(
            src_ref=src, dst_ref=dst, send_sem=ss.at[kind, c], recv_sem=rs.at[kind, c],
            device_id=dev, device_id_type=MESH,
        )

    def tok_msg(slot, src, dev):
        return pltpu.make_async_remote_copy(
            src_ref=src, dst_ref=gat.at[slot], send_sem=ts.at[slot], recv_sem=tr.at[slot],
            device_id=dev, device_id_type=MESH,
        )

    def in_place(name, c, rows, cols, dev):
        ref = hh.at[c, :, rows, cols]
        return msg(name, c, ref, ref, dev)

    own_a, mate_a = cols_of(w * KA, OA), cols_of((1 - w) * KA, OA)
    out_a, in_a = cols_of(w * OA, KA), cols_of((1 - w) * OA, KA)
    own_b, mate_b = cols_of(CA + w * KB, OB), cols_of(CA + (1 - w) * KB, OB)
    own_b_left = cols_of(CA + w * KB, OL)
    own_b_right = cols_of(CA + w * KB + OL, OR)
    out_b, in_b = cols_of(CA + w * OB, KB), cols_of(CA + (1 - w) * OB, KB)
    all_a, lo_a, hi_a = pl.ds(0, CA), pl.ds(0, OA), pl.ds(OA, KA)

    def m_core(c, k):
        return msg(f"core{k}", c, cs.at[c % 2, k], cr.at[c % 3, k], core)

    def m_x1p(c):
        return msg("x1p", c, x1s.at[c, :, :, lo_a], x1a.at[c], right)

    def m_x1m(c):
        return msg("x1m", c, x1s.at[c, :, :, hi_a], x1b.at[c], left)

    def m_x2p(c):
        return msg("x2p", c, x2s.at[c, 0], x2r.at[c, 0], right)

    def m_x2m(c):
        return msg("x2m", c, x2s.at[c, 1], x2r.at[c, 1], left)

    def m_zred(c):
        return msg("zred", c, zs.at[c], zr.at[c], zmate)

    def m_zgat(c, cols):
        return in_place("zgat", c, rows_of(x), cols, zmate)

    def m_g1p(c, xx):
        return in_place("g1p", c, rows_of(xx), all_a, right)

    def m_g1m(c, xx):
        return in_place("g1m", c, rows_of(xx), all_a, left)

    def m_g2p(c, xx):
        return in_place("g2p", c, rows_of(xx), hi_a, right)

    def m_g2m(c, xx):
        return in_place("g2m", c, rows_of(xx), lo_a, left)

    def m_y0(c):
        return msg("y0", c, y0s.at[c], y0r.at[c], zmate)

    def m_y1p(c):
        return msg("y1p", c, y1s.at[c, :, :, :OL], y1a.at[c], right)

    def m_y1m(c):
        return msg("y1m", c, y1s.at[c, :, :, OL:], y1b.at[c], left)

    def m_y2p(c):
        return msg("y2p", c, y2s.at[c, 0], y2r.at[c, 0], right)

    def m_y2m(c):
        return msg("y2m", c, y2s.at[c, 1], y2r.at[c, 1], left)

    def m_k1p(c, xx):
        return in_place("k1p", c, rows_of(xx), own_b, right)

    def m_k1m(c, xx):
        return in_place("k1m", c, rows_of(xx), own_b, left)

    def m_k2p(c, xx):
        return in_place("k2p", c, rows_of(xx), own_b_right, right)

    def m_k2m(c, xx):
        return in_place("k2m", c, rows_of(xx), own_b_left, left)

    def m_k3(c, cols):
        return in_place("k3", c, half_of(q), cols, zmate)

    def m_cgat(c, qq):
        ref = hh.at[c, :, half_of(qq), :]
        return msg("cgat", c, ref, ref, core)

    def m_mix(c):
        dy = jnp.where(c >= 6, 2, c % 3 + c % 3 // 2)
        return msg("mix", c, ms.at[c], mr.at[c], tdev(dy, 0))

    def m_far():
        return msg("mix", 0, ms.at[0], mr.at[0], tdev(0, 1))

    for s in (1, 2, 3):
        dy, dh = offsets[s]
        tok_msg(s, gat.at[0], tdev(-dy % 4, dh)).start()
    for copy in weights:
        copy.wait()

    def a_partials(c):
        @pl.when((c != 0) & (c != 3))
        def _():
            tok_msg(c, gat.at[0], core).wait_recv()

        both = jnp.concatenate([gat[c, half_of(1 - q), :], gat[c, half_of(q), :]], axis=0)
        tok, sc = both[:, :WIDTH], both[:, WIDTH:]
        for k, mat in enumerate((wg, wu, wd)):
            for n0, nw in DOT_COLUMNS:
                cols = slice(n0, n0 + nw)
                if k < 2:
                    part = jnp.dot(tok, mat[:, cols], preferred_element_type=F32)
                else:
                    part = lax.dot_general(
                        sc, mat[cols, :], (((1,), (1,)), ((), ())), preferred_element_type=F32
                    )
                cs[c % 2, k, :, cols] = part[:HALF]
                acc[c % 5, k, :, cols] = part[HALF:]
            m_core(c, k).start()

    def forward_tokens():
        tok_msg(3, gat.at[0], core).wait_recv()
        for s in (4, 5):
            tok_msg(s, gat.at[3], tdev(-offsets[s][0] % 4, 0)).start()

    def send_far_tokens():
        tok_msg(6, gat.at[3], tdev(2, 0)).start()
        tok_msg(7, gat.at[0], tdev(2, 0)).start()

    def b_stage(c):
        a = c % 5
        for k in range(3):
            m_core(c, k).wait_recv()
        acc[a] += cr[c % 3]
        x1s[c] = acc[a, :, seg_of(xo), :CA].astype(BF16)
        m_x1p(c).start()
        m_x1m(c).start()
        y0s[c] = acc[a, :, :, mate_b].astype(BF16)
        m_y0(c).start()
        for k in range(3):
            m_core(c, k).wait_send()

    def c_stage(c):
        a = c % 5
        m_x1p(c).wait_recv()
        m_x1m(c).wait_recv()
        acc[a, :, seg_of(xp), :OA] += x1a[c].astype(F32)
        acc[a, :, seg_of(xm), OA:CA] += x1b[c].astype(F32)
        x2s[c, 0] = acc[a, :, seg_of(xp), :CA].astype(BF16)
        x2s[c, 1] = acc[a, :, seg_of(xm), :CA].astype(BF16)
        m_x2p(c).start()
        m_x2m(c).start()

    def c2_stage(c):
        a = c % 5
        m_y0(c).wait_recv()
        acc[a, :, :, own_b] += y0r[c].astype(F32)
        y1s[c] = acc[a, :, seg_of(xo), own_b].astype(BF16)
        m_y1p(c).start()
        m_y1m(c).start()

    def d_stage(c):
        a = c % 5
        m_x2p(c).wait_recv()
        m_x2m(c).wait_recv()
        acc[a, :, seg_of(x), :CA] += x2r[c, 0].astype(F32) + x2r[c, 1].astype(F32)
        zs[c] = acc[a, :, seg_of(x), mate_a].astype(BF16)
        m_zred(c).start()

    def d2_stage(c):
        a = c % 5
        m_y1p(c).wait_recv()
        m_y1m(c).wait_recv()
        acc[a, :, seg_of(xp), own_b_left] += y1a[c].astype(F32)
        acc[a, :, seg_of(xm), own_b_right] += y1b[c].astype(F32)
        y2s[c, 0] = acc[a, :, seg_of(xp), own_b].astype(BF16)
        y2s[c, 1] = acc[a, :, seg_of(xm), own_b].astype(BF16)
        m_y2p(c).start()
        m_y2m(c).start()

    def finish_units(c, tot, cols):
        gate, up, dhid = tot[0], tot[1], tot[2]
        sig = jax.nn.sigmoid(gate)
        hh[c, 0, rows_of(x), cols] = (gate * sig * up).astype(BF16)
        hh[c, 1, rows_of(x), cols] = (dhid * up * sig * (1.0 + gate * (1.0 - sig))).astype(BF16)
        hh[c, 2, rows_of(x), cols] = (dhid * gate * sig).astype(BF16)

    def e_stage(c):
        a = c % 5
        m_zred(c).wait_recv()
        finish_units(c, acc[a, :, seg_of(x), own_a] + zr[c].astype(F32), own_a)
        m_zgat(c, out_a).start()

    def e2_stage(c):
        a = c % 5
        m_y2p(c).wait_recv()
        m_y2m(c).wait_recv()
        tot = acc[a, :, seg_of(x), own_b] + y2r[c, 0].astype(F32) + y2r[c, 1].astype(F32)
        finish_units(c, tot, own_b)
        m_k1p(c, x).start()
        m_k1m(c, x).start()

    def f_stage(c):
        m_zgat(c, in_a).wait_recv()
        m_g1p(c, x).start()
        m_g1m(c, x).start()

    def f2_stage(c):
        m_k1p(c, xm).wait_recv()
        m_k2p(c, xm).start()
        m_k1m(c, xp).wait_recv()
        m_k2m(c, xp).start()

    def g_stage(c):
        m_g1p(c, xm).wait_recv()
        m_g2p(c, xm).start()
        m_g1m(c, xp).wait_recv()
        m_g2m(c, xp).start()

    def g2_stage(c):
        m_k2p(c, xo).wait_recv()
        m_k2m(c, xo).wait_recv()
        m_k3(c, out_b).start()

    def h_stage(c):
        m_g2p(c, xo).wait_recv()
        m_g2m(c, xo).wait_recv()
        m_k3(c, in_b).wait_recv()
        m_cgat(c, q).start()

    def i_stage(c):
        m_cgat(c, 1 - q).wait_recv()
        part = jnp.dot(hh[c, 0], wd[...], preferred_element_type=F32)

        @pl.when(c == 0)
        def _():
            mown[...] = part

        @pl.when(c == 3)
        def _():
            mfar[...] = part

        @pl.when((c != 0) & (c != 3))
        def _():
            ms[c] = part.astype(BF16)
            m_mix(c).start()

        tokens_c = cols_of(c * ROWS, ROWS)
        hidt[:, tokens_c] = hh[c, 0].T
        tokt[:, tokens_c] = gat[c, :, :WIDTH].T

    def join_mixed():
        for c in (4, 5, 6):
            m_mix(c).wait_recv()
            mfar[...] += mr[c].astype(F32)
        ms[0] = mfar[...].astype(BF16)
        m_far().start()

    plan = [
        (e_stage, 5, False), (c_stage, 2, False), (g2_stage, 8, True), (g_stage, 11, True),
        (f_stage, 9, True), (b_stage, 1, False), (d_stage, 3, False), (f2_stage, 6, True),
        (a_partials, 0, False), (h_stage, 12, True), (e2_stage, 4, False), (c2_stage, 2, False),
        (d2_stage, 3, False), (i_stage, 13, True),
    ]
    last = max(lag for _, lag, _ in plan)

    def step(i, carry):
        for stage, lag, back in plan:
            j = i - lag
            c = (j + 1) % SLOTS if back else j

            @pl.when((j >= 0) & (j < SLOTS))
            def _(stage=stage, c=c):
                stage(c)

        @pl.when(i == 1)
        def _():
            forward_tokens()

        @pl.when(i == 2)
        def _():
            send_far_tokens()

        @pl.when(i == JOIN)
        def _():
            join_mixed()

        return carry

    lax.fori_loop(0, SLOTS + last, step, 0)

    for c in (1, 2, 7):
        m_mix(c).wait_recv()
        mown[...] += mr[c].astype(F32)
    m_far().wait_recv()
    mown[...] += mr[0].astype(F32)

    def drain(c, carry):
        for message in (
            m_x1p(c), m_x1m(c), m_x2p(c), m_x2m(c), m_zred(c), m_zgat(c, out_a),
            m_g1p(c, x), m_g1m(c, x), m_g2p(c, xm), m_g2m(c, xp), m_cgat(c, q),
            m_y0(c), m_y1p(c), m_y1m(c), m_y2p(c), m_y2m(c), m_k1p(c, x), m_k1m(c, x),
            m_k2p(c, xm), m_k2m(c, xp), m_k3(c, out_b),
        ):
            message.wait_send()

        @pl.when(c != 3)
        def _():
            m_mix(c).wait_send()

        @pl.when(c != 0)
        def _():
            tok_msg(c, gat.at[0], core).wait_send()

        return carry

    lax.fori_loop(0, SLOTS, drain, 0)


def exchange(ids, tokens, grad_out, wg, wu, wd):
    vmem = pl.BlockSpec(memory_space=pltpu.VMEM)
    hbm = pl.BlockSpec(memory_space=pltpu.HBM)
    total = SLOTS * ROWS
    kinds = len(NAMES)
    return pl.pallas_call(
        exchange_kernel,
        name="exchange",
        out_shape=(
            pltpu.VMEM((ROWS, WIDTH), F32),
            pltpu.VMEM((SLOTS, ROWS, 2 * WIDTH), BF16),
            pltpu.VMEM((WIDTH, total), BF16),
            pltpu.VMEM((UNITS, total), BF16),
            pltpu.VMEM((SLOTS, 3, ROWS, UNITS), BF16),
        ),
        in_specs=[hbm] * 6,
        out_specs=(vmem,) * 5,
        scratch_shapes=[
            pltpu.VMEM((SLOTS, ROWS), jnp.int32),
            pltpu.VMEM((ROWS, WIDTH), BF16),
            pltpu.VMEM((WIDTH, UNITS), BF16),
            pltpu.VMEM((WIDTH, UNITS), BF16),
            pltpu.VMEM((UNITS, WIDTH), BF16),
            pltpu.VMEM((5, 3, HALF, UNITS), F32),
            pltpu.VMEM((2, 3, HALF, UNITS), F32),
            pltpu.VMEM((3, 3, HALF, UNITS), F32),
            pltpu.VMEM((SLOTS, 3, SEG, CA), BF16),
            pltpu.VMEM((SLOTS, 3, SEG, OA), BF16),
            pltpu.VMEM((SLOTS, 3, SEG, KA), BF16),
            pltpu.VMEM((SLOTS, 2, 3, SEG, CA), BF16),
            pltpu.VMEM((SLOTS, 2, 3, SEG, CA), BF16),
            pltpu.VMEM((SLOTS, 3, SEG, OA), BF16),
            pltpu.VMEM((SLOTS, 3, SEG, OA), BF16),
            pltpu.VMEM((SLOTS, 3, HALF, OB), BF16),
            pltpu.VMEM((SLOTS, 3, HALF, OB), BF16),
            pltpu.VMEM((SLOTS, 3, SEG, OB), BF16),
            pltpu.VMEM((SLOTS, 3, SEG, OL), BF16),
            pltpu.VMEM((SLOTS, 3, SEG, OR), BF16),
            pltpu.VMEM((SLOTS, 2, 3, SEG, OB), BF16),
            pltpu.VMEM((SLOTS, 2, 3, SEG, OB), BF16),
            pltpu.VMEM((SLOTS, ROWS, WIDTH), BF16),
            pltpu.VMEM((SLOTS, ROWS, WIDTH), BF16),
            pltpu.VMEM((ROWS, WIDTH), F32),
            pltpu.SemaphoreType.DMA((kinds, SLOTS)),
            pltpu.SemaphoreType.DMA((kinds, SLOTS)),
            pltpu.SemaphoreType.DMA((SLOTS,)),
            pltpu.SemaphoreType.DMA((SLOTS,)),
            pltpu.SemaphoreType.DMA((3,)),
            pltpu.SemaphoreType.DMA((3,)),
        ],
        compiler_params=pltpu.CompilerParams(
            collective_id=0, has_side_effects=True, vmem_limit_bytes=35 * 2**20
        ),
        cost_estimate=pl.CostEstimate(
            flops=8 * total * WIDTH * UNITS, bytes_accessed=24 * 2**20, transcendentals=0
        ),
    )(ids, tokens, grad_out, wg, wu, wd)


GRAD_COLUMNS = 640


def grads_kernel(
    mown, gat, tokt, hidt, hh, mixed, grad_gate, grad_up, grad_down,
    mbuf, gbuf, ubuf, dbuf, sems, msem,
):
    total = SLOTS * ROWS
    mbuf[...] = mown[...].astype(BF16)
    mcopy = pltpu.make_async_copy(mbuf, mixed, msem)
    mcopy.start()
    tok_t = tokt[...]
    sc = gat[:, :, WIDTH:].reshape(total, WIDTH)
    blocks = []
    for n in range(UNITS // GRAD_COLUMNS):
        cols = pl.ds(n * GRAD_COLUMNS, GRAD_COLUMNS)
        slot = n % 2
        copies = [
            pltpu.make_async_copy(gbuf.at[slot], grad_gate.at[:, cols], sems.at[0, slot]),
            pltpu.make_async_copy(ubuf.at[slot], grad_up.at[:, cols], sems.at[1, slot]),
            pltpu.make_async_copy(dbuf.at[slot], grad_down.at[cols, :], sems.at[2, slot]),
        ]
        blocks.append(copies)
        for k, buf in enumerate((gbuf, ubuf, dbuf)):
            if n >= 2:
                blocks[n - 2][k].wait()
            if k < 2:
                right = hh[:, k + 1, :, cols].reshape(total, GRAD_COLUMNS)
                buf[slot] = jnp.dot(tok_t, right, preferred_element_type=F32)
            else:
                buf[slot] = jnp.dot(hidt[cols, :], sc, preferred_element_type=F32)
            copies[k].start()
    for copies in blocks[-2:]:
        for copy in copies:
            copy.wait()
    mcopy.wait()


def grads(mown, gat, tokt, hidt, hh):
    total = SLOTS * ROWS
    vmem = pl.BlockSpec(memory_space=pltpu.VMEM)
    hbm = pl.BlockSpec(memory_space=pl.ANY)
    return pl.pallas_call(
        grads_kernel,
        name="grads",
        out_shape=(
            jax.ShapeDtypeStruct((ROWS, WIDTH), BF16),
            jax.ShapeDtypeStruct((WIDTH, UNITS), F32),
            jax.ShapeDtypeStruct((WIDTH, UNITS), F32),
            jax.ShapeDtypeStruct((UNITS, WIDTH), F32),
        ),
        in_specs=[vmem] * 5,
        out_specs=(hbm,) * 4,
        scratch_shapes=[
            pltpu.VMEM((ROWS, WIDTH), BF16),
            pltpu.VMEM((2, WIDTH, GRAD_COLUMNS), F32),
            pltpu.VMEM((2, WIDTH, GRAD_COLUMNS), F32),
            pltpu.VMEM((2, GRAD_COLUMNS, WIDTH), F32),
            pltpu.SemaphoreType.DMA((3, 2)),
            pltpu.SemaphoreType.DMA,
        ],
        compiler_params=pltpu.CompilerParams(vmem_limit_bytes=32 * 2**20),
        cost_estimate=pl.CostEstimate(
            flops=6 * total * WIDTH * UNITS, bytes_accessed=12 * 2**20, transcendentals=0
        ),
    )(mown, gat, tokt, hidt, hh)


def shards(tokens, segment_ids, gate_weight, up_weight, down_weight, grad_out):
    ids = segment_ids.reshape(SLOTS, ROWS)
    arrays = (ids, tokens, grad_out, gate_weight, up_weight, down_weight)
    outs = exchange(*(pltpu.with_memory_space_constraint(a, pltpu.HBM) for a in arrays))
    return grads(*outs)


def solution(mesh):
    placed = (
        P("tensor", "dp"),
        P(),
        P("dp", "tensor"),
        P("dp", "tensor"),
        P("tensor", "dp"),
        P("tensor", "dp"),
    )
    return jax.shard_map(
        shards,
        mesh=mesh,
        in_specs=placed,
        out_specs=(P("tensor", "dp"), P("dp", "tensor"), P("dp", "tensor"), P("tensor", "dp")),
        check_vma=False,
    )
```

```python
import jax
import jax.numpy as jnp
from jax import lax
from jax.experimental import pallas as pl
from jax.experimental.pallas import tpu as pltpu
from jax.sharding import PartitionSpec as P

NSEG = 8
SLOTS = 8
ROWS = 128
HALF = 64
SEG = 16
OWN, MATE = 7, 1
WIDTH = 512
UNITS = 1920
TILE = 128
MESH = pl.DeviceIdType.MESH
BF16 = jnp.bfloat16
F32 = jnp.float32
DOT_COLUMNS = ((0, 512), (512, 512), (1024, 512), (1536, 384))

JOIN = 18
EARLY = 4
EARLY_STEPS = (17, 18)

CA = 1152
CB = UNITS - CA
OA = -(-CA // (2 * TILE)) * TILE
KA = CA - OA
OB = -(-CB // (2 * TILE)) * TILE
KB = CB - OB
OL = OB // (2 * TILE) * TILE
OR = OB - OL

DEPTH = 4
NAMES = (
    "core0", "core1", "core2", "x1p", "x1m", "x2p", "x2m", "zred", "zgat", "g1p", "g1m", "g2p", "g2m", "cgat",
    "mix", "y0", "y1p", "y1m", "y2p", "y2m", "k1p", "k1m", "k2p", "k2m", "k3",
)
KIND = {name: i for i, name in enumerate(NAMES)}


def exchange_kernel(
    ids_hbm, tokens_hbm, grad_out_hbm, wg_hbm, wu_hbm, wd_hbm,
    mown, gat, tokt, hidt, hh, early,
    ids, grad_out, wg, wu, wd, acc, cs, cr, x1s, x1a, x1b, x2s, x2r, zs, zr,
    y0s, y0r, y1s, y1a, y1b, y2s, y2r, ms, mr, mfr, mfar,
    ss, rs, ts, tr, ws, own_sems,
):
    inputs = [
        pltpu.make_async_copy(a, b, own_sems.at[k])
        for k, (a, b) in enumerate(
            ((ids_hbm, ids), (grad_out_hbm, grad_out), (tokens_hbm, gat.at[OWN, :, :WIDTH]))
        )
    ]
    for copy in inputs:
        copy.start()
    weights = [
        pltpu.make_async_copy(a, b, ws.at[k])
        for k, (a, b) in enumerate(((wg_hbm, wg), (wu_hbm, wu), (wd_hbm, wd)))
    ]
    for copy in weights:
        copy.start()

    dp = lax.axis_index("dp")
    tn = lax.axis_index("tensor")
    w, x, q = dp // 8, (dp // 2) % 4, dp % 2
    y, h = tn // 2, tn % 2
    xp, xm, xo = (x + 1) % 4, (x + 3) % 4, (x + 2) % 4

    def dpdev(w=w, x=x, q=q):
        return (w * 8 + x * 2 + q, tn)

    def tdev(dy, dh):
        return (dp, ((y + dy) % 4) * 2 + (h + dh) % 2)

    core, right, left, zmate = dpdev(q=1 - q), dpdev(x=xp), dpdev(x=xm), dpdev(w=1 - w)
    offsets = [(1, 0), (0, 1), (1, 1), (3, 1), (2, 1), (3, 0), (2, 0), (0, 0)]

    barrier = pltpu.get_barrier_semaphore()
    partners = [core, right, left, zmate] + [tdev(*o) for o in offsets[:OWN]]
    for p in partners:
        pl.semaphore_signal(barrier, inc=1, device_id=p, device_id_type=MESH)

    for copy in inputs:
        copy.wait()
    all_ids = ids[...]
    own_ids = ids[pl.ds(tn, 1), :]
    row = jnp.zeros((1, ROWS), F32)
    for s in range(NSEG):
        length = jnp.sum(jnp.where(all_ids == s, 1.0, 0.0), axis=(0, 1), keepdims=True)
        row = jnp.where(own_ids == s, lax.rsqrt(length), row)
    square = jnp.broadcast_to(row, (ROWS, ROWS))
    on_diagonal = lax.broadcasted_iota(jnp.int32, (ROWS, ROWS), 0) == lax.broadcasted_iota(
        jnp.int32, (ROWS, ROWS), 1
    )
    column = jnp.sum(jnp.where(on_diagonal, square, 0.0), axis=1, keepdims=True)
    gat[OWN, :, WIDTH:] = (grad_out[...].astype(F32) * column).astype(BF16)

    pl.semaphore_wait(barrier, len(partners))

    def rows_of(xx):
        return pl.ds(pl.multiple_of(q * HALF + xx * SEG, SEG), SEG)

    def seg_of(xx):
        return pl.ds(pl.multiple_of(xx * SEG, SEG), SEG)

    def half_of(qq):
        return pl.ds(pl.multiple_of(qq * HALF, HALF), HALF)

    def cols_of(start, size):
        return pl.ds(pl.multiple_of(start, TILE), size)

    def msg(name, c, src, dst, dev):
        kind = KIND[name]
        return pltpu.make_async_remote_copy(
            src_ref=src, dst_ref=dst, send_sem=ss.at[kind, c], recv_sem=rs.at[kind, c],
            device_id=dev, device_id_type=MESH,
        )

    def tok_msg(slot, src, dev):
        return pltpu.make_async_remote_copy(
            src_ref=src, dst_ref=gat.at[slot], send_sem=ts.at[slot], recv_sem=tr.at[slot],
            device_id=dev, device_id_type=MESH,
        )

    def in_place(name, c, rows, cols, dev):
        ref = hh.at[c, :, rows, cols]
        return msg(name, c, ref, ref, dev)

    own_a, mate_a = cols_of(w * KA, OA), cols_of((1 - w) * KA, OA)
    out_a, in_a = cols_of(w * OA, KA), cols_of((1 - w) * OA, KA)
    own_b, mate_b = cols_of(CA + w * KB, OB), cols_of(CA + (1 - w) * KB, OB)
    own_b_left = cols_of(CA + w * KB, OL)
    own_b_right = cols_of(CA + w * KB + OL, OR)
    out_b, in_b = cols_of(CA + w * OB, KB), cols_of(CA + (1 - w) * OB, KB)
    all_a, lo_a, hi_a = pl.ds(0, CA), pl.ds(0, OA), pl.ds(OA, KA)

    def m_core(c, k):
        return msg(f"core{k}", c, cs.at[c % 2, k], cr.at[c % 2, k], core)

    def m_x1p(c):
        return msg("x1p", c, x1s.at[c % DEPTH, :, :, lo_a], x1a.at[c % DEPTH], right)

    def m_x1m(c):
        return msg("x1m", c, x1s.at[c % DEPTH, :, :, hi_a], x1b.at[c % DEPTH], left)

    def m_x2p(c):
        return msg("x2p", c, x2s.at[c % DEPTH, 0], x2r.at[c % DEPTH, 0], right)

    def m_x2m(c):
        return msg("x2m", c, x2s.at[c % DEPTH, 1], x2r.at[c % DEPTH, 1], left)

    def m_zred(c):
        return msg("zred", c, zs.at[c % DEPTH], zr.at[c % DEPTH], zmate)

    def m_zgat(c, cols):
        return in_place("zgat", c, rows_of(x), cols, zmate)

    def m_g1p(c, xx):
        return in_place("g1p", c, rows_of(xx), all_a, right)

    def m_g1m(c, xx):
        return in_place("g1m", c, rows_of(xx), all_a, left)

    def m_g2p(c, xx):
        return in_place("g2p", c, rows_of(xx), hi_a, right)

    def m_g2m(c, xx):
        return in_place("g2m", c, rows_of(xx), lo_a, left)

    def m_y0(c):
        return msg("y0", c, y0s.at[c % DEPTH], y0r.at[c % DEPTH], zmate)

    def m_y1p(c):
        return msg("y1p", c, y1s.at[c % DEPTH, :, :, :OL], y1a.at[c % DEPTH], right)

    def m_y1m(c):
        return msg("y1m", c, y1s.at[c % DEPTH, :, :, OL:], y1b.at[c % DEPTH], left)

    def m_y2p(c):
        return msg("y2p", c, y2s.at[c % DEPTH, 0], y2r.at[c % DEPTH, 0], right)

    def m_y2m(c):
        return msg("y2m", c, y2s.at[c % DEPTH, 1], y2r.at[c % DEPTH, 1], left)

    def m_k1p(c, xx):
        return in_place("k1p", c, rows_of(xx), own_b, right)

    def m_k1m(c, xx):
        return in_place("k1m", c, rows_of(xx), own_b, left)

    def m_k2p(c, xx):
        return in_place("k2p", c, rows_of(xx), own_b_right, right)

    def m_k2m(c, xx):
        return in_place("k2m", c, rows_of(xx), own_b_left, left)

    def m_k3(c, cols):
        return in_place("k3", c, half_of(q), cols, zmate)

    def m_cgat(c, qq):
        ref = hh.at[c, :, half_of(qq), :]
        return msg("cgat", c, ref, ref, core)

    def m_mix(c):
        dy = jnp.where(c == 0, 1, jnp.where(c % 2 == 1, 3, jnp.where(c == 2, 1, 2)))
        return msg("mix", c, ms.at[c], mr.at[c], tdev(dy, 0))

    def m_far():
        return msg("mix", OWN, mfar, mfr, tdev(0, 1))

    for s in (0, 5, MATE):
        dy, dh = offsets[s]
        tok_msg(s, gat.at[OWN], tdev(-dy % 4, dh)).start()
    for copy in weights:
        copy.wait()

    def a_partials(c, r):
        @pl.when((c != OWN) & (c != MATE))
        def _():
            tok_msg(c, gat.at[OWN], core).wait_recv()

        both = jnp.concatenate([gat[c, half_of(1 - q), :], gat[c, half_of(q), :]], axis=0)
        tok, sc = both[:, :WIDTH], both[:, WIDTH:]
        for k, mat in enumerate((wg, wu, wd)):
            for n0, nw in DOT_COLUMNS:
                cols = slice(n0, n0 + nw)
                if k < 2:
                    part = jnp.dot(tok, mat[:, cols], preferred_element_type=F32)
                else:
                    part = lax.dot_general(
                        sc, mat[cols, :], (((1,), (1,)), ((), ())), preferred_element_type=F32
                    )
                cs[r % 2, k, :, cols] = part[:HALF]
                acc[r % 5, k, :, cols] = part[HALF:]
            m_core(r, k).start()

    def forward_tokens():
        tok_msg(MATE, gat.at[OWN], core).wait_recv()
        for s in (2, 3):
            tok_msg(s, gat.at[MATE], tdev(-offsets[s][0] % 4, 0)).start()

    def send_far_tokens():
        tok_msg(4, gat.at[MATE], tdev(2, 0)).start()
        tok_msg(6, gat.at[OWN], tdev(2, 0)).start()

    def b_stage(c, r):
        a = r % 5
        for k in range(3):
            m_core(r, k).wait_recv()
        acc[a] += cr[r % 2]
        x1s[r % DEPTH] = acc[a, :, seg_of(xo), :CA].astype(BF16)
        m_x1p(r).start()
        m_x1m(r).start()
        y0s[r % DEPTH] = acc[a, :, :, mate_b].astype(BF16)
        m_y0(r).start()
        for k in range(3):
            m_core(r, k).wait_send()

    def c_stage(c, r):
        a = r % 5
        m_x1p(r).wait_recv()
        m_x1m(r).wait_recv()
        acc[a, :, seg_of(xp), :OA] += x1a[r % DEPTH].astype(F32)
        acc[a, :, seg_of(xm), OA:CA] += x1b[r % DEPTH].astype(F32)
        x2s[r % DEPTH, 0] = acc[a, :, seg_of(xp), :CA].astype(BF16)
        x2s[r % DEPTH, 1] = acc[a, :, seg_of(xm), :CA].astype(BF16)
        m_x2p(r).start()
        m_x2m(r).start()

    def c2_stage(c, r):
        a = r % 5
        m_y0(r).wait_recv()
        acc[a, :, :, own_b] += y0r[r % DEPTH].astype(F32)
        y1s[r % DEPTH] = acc[a, :, seg_of(xo), own_b].astype(BF16)
        m_y1p(r).start()
        m_y1m(r).start()

    def d_stage(c, r):
        a = r % 5
        m_x2p(r).wait_recv()
        m_x2m(r).wait_recv()
        acc[a, :, seg_of(x), :CA] += x2r[r % DEPTH, 0].astype(F32) + x2r[r % DEPTH, 1].astype(F32)
        zs[r % DEPTH] = acc[a, :, seg_of(x), mate_a].astype(BF16)
        m_zred(r).start()

    def d2_stage(c, r):
        a = r % 5
        m_y1p(r).wait_recv()
        m_y1m(r).wait_recv()
        acc[a, :, seg_of(xp), own_b_left] += y1a[r % DEPTH].astype(F32)
        acc[a, :, seg_of(xm), own_b_right] += y1b[r % DEPTH].astype(F32)
        y2s[r % DEPTH, 0] = acc[a, :, seg_of(xp), own_b].astype(BF16)
        y2s[r % DEPTH, 1] = acc[a, :, seg_of(xm), own_b].astype(BF16)
        m_y2p(r).start()
        m_y2m(r).start()

    def finish_units(c, tot, cols):
        gate, up, dhid = tot[0], tot[1], tot[2]
        sig = jax.nn.sigmoid(gate)
        hh[c, 0, rows_of(x), cols] = (gate * sig * up).astype(BF16)
        hh[c, 1, rows_of(x), cols] = (dhid * up * sig * (1.0 + gate * (1.0 - sig))).astype(BF16)
        hh[c, 2, rows_of(x), cols] = (dhid * gate * sig).astype(BF16)

    def e_stage(c, r):
        a = r % 5
        for message in (m_x1p(r), m_x1m(r), m_x2p(r), m_x2m(r), m_zred(r)):
            message.wait_send()
        m_zred(r).wait_recv()
        finish_units(c, acc[a, :, seg_of(x), own_a] + zr[r % DEPTH].astype(F32), own_a)
        m_zgat(c, out_a).start()

    def e2_stage(c, r):
        a = r % 5
        for message in (m_y0(r), m_y1p(r), m_y1m(r), m_y2p(r), m_y2m(r)):
            message.wait_send()
        m_y2p(r).wait_recv()
        m_y2m(r).wait_recv()
        tot = acc[a, :, seg_of(x), own_b] + y2r[r % DEPTH, 0].astype(F32) + y2r[r % DEPTH, 1].astype(F32)
        finish_units(c, tot, own_b)
        m_k1p(c, x).start()
        m_k1m(c, x).start()

    def f_stage(c):
        m_zgat(c, in_a).wait_recv()
        m_g1p(c, x).start()
        m_g1m(c, x).start()

    def f2_stage(c):
        m_k1p(c, xm).wait_recv()
        m_k2p(c, xm).start()
        m_k1m(c, xp).wait_recv()
        m_k2m(c, xp).start()

    def g_stage(c):
        m_g1p(c, xm).wait_recv()
        m_g2p(c, xm).start()
        m_g1m(c, xp).wait_recv()
        m_g2m(c, xp).start()

    def g2_stage(c):
        m_k2p(c, xo).wait_recv()
        m_k2m(c, xo).wait_recv()
        m_k3(c, out_b).start()

    def h_stage(c):
        m_g2p(c, xo).wait_recv()
        m_g2m(c, xo).wait_recv()
        m_k3(c, in_b).wait_recv()
        m_cgat(c, q).start()

    def i_stage(c):
        m_cgat(c, 1 - q).wait_recv()
        part = jnp.dot(hh[c, 0], wd[...], preferred_element_type=F32)

        @pl.when(c == OWN)
        def _():
            mown[...] = part

        @pl.when(c == MATE)
        def _():
            mfar[...] = part

        @pl.when((c != OWN) & (c != MATE))
        def _():
            ms[c] = part.astype(BF16)
            m_mix(c).start()

        tokens_c = cols_of(c * ROWS, ROWS)
        hidt[:, tokens_c] = hh[c, 0].T
        tokt[:, tokens_c] = gat[c, :, :WIDTH].T

    def join_mixed():
        for c in (2, 3, 4):
            m_mix(c).wait_recv()
            mfar[...] += mr[c].astype(F32)
        m_far().start()

    def early_gradient(k):
        depth = EARLY * ROWS
        for n0, nw in DOT_COLUMNS:
            block = pl.ds(n0, nw)
            right = hh[:EARLY, k + 1, :, block].reshape(depth, nw)
            early[k, :, block] = jnp.dot(tokt[:, :depth], right, preferred_element_type=F32)

    plan = [
        (e_stage, 5, False), (c_stage, 2, False), (g2_stage, 9, True), (g_stage, 11, True),
        (f_stage, 9, True), (b_stage, 1, False), (d_stage, 3, False), (f2_stage, 7, True),
        (a_partials, 0, False), (h_stage, 12, True), (e2_stage, 4, False), (c2_stage, 2, False),
        (d2_stage, 3, False), (i_stage, 13, True),
    ]
    last = max(lag for _, lag, _ in plan)

    def step(i, carry):
        for stage, lag, back in plan:
            j = i - lag
            @pl.when((j >= 0) & (j < SLOTS))
            def _(stage=stage, j=j, back=back):
                if back:
                    stage(j)
                else:
                    slot = jnp.where(j == 0, OWN, jnp.where(j == 1, 0, jnp.where(j == 2, 5, j - 2)))
                    stage(jnp.where(j == 7, 6, slot), j)

        @pl.when(i == 1)
        def _():
            forward_tokens()

        @pl.when(i == 2)
        def _():
            send_far_tokens()

        @pl.when(i == JOIN)
        def _():
            join_mixed()

        for k, at in enumerate(EARLY_STEPS):

            @pl.when(i == at)
            def _(k=k):
                early_gradient(k)

        return carry

    lax.fori_loop(0, SLOTS + last, step, 0)

    for c in (0, 5, 6):
        m_mix(c).wait_recv()
        mown[...] += mr[c].astype(F32)
    m_far().wait_recv()
    mown[...] += mfr[...]

    def drain(c, carry):
        for message in (
            m_zgat(c, out_a), m_g1p(c, x), m_g1m(c, x), m_g2p(c, xm), m_g2m(c, xp),
            m_cgat(c, q), m_k1p(c, x), m_k1m(c, x), m_k2p(c, xm), m_k2m(c, xp), m_k3(c, out_b),
        ):
            message.wait_send()

        @pl.when((c != OWN) & (c != MATE))
        def _():
            m_mix(c).wait_send()

        @pl.when(c != OWN)
        def _():
            tok_msg(c, gat.at[OWN], core).wait_send()

        return carry

    lax.fori_loop(0, SLOTS, drain, 0)
    m_far().wait_send()


def exchange(ids, tokens, grad_out, wg, wu, wd):
    vmem = pl.BlockSpec(memory_space=pltpu.VMEM)
    hbm = pl.BlockSpec(memory_space=pltpu.HBM)
    total = SLOTS * ROWS
    kinds = len(NAMES)
    return pl.pallas_call(
        exchange_kernel,
        name="exchange",
        out_shape=(
            pltpu.VMEM((ROWS, WIDTH), F32),
            pltpu.VMEM((SLOTS, ROWS, 2 * WIDTH), BF16),
            pltpu.VMEM((WIDTH, total), BF16),
            pltpu.VMEM((UNITS, total), BF16),
            pltpu.VMEM((SLOTS, 3, ROWS, UNITS), BF16),
            pltpu.VMEM((len(EARLY_STEPS), WIDTH, UNITS), F32),
        ),
        in_specs=[hbm] * 6,
        out_specs=(vmem,) * 6,
        scratch_shapes=[
            pltpu.VMEM((SLOTS, ROWS), jnp.int32),
            pltpu.VMEM((ROWS, WIDTH), BF16),
            pltpu.VMEM((WIDTH, UNITS), BF16),
            pltpu.VMEM((WIDTH, UNITS), BF16),
            pltpu.VMEM((UNITS, WIDTH), BF16),
            pltpu.VMEM((5, 3, HALF, UNITS), F32),
            pltpu.VMEM((2, 3, HALF, UNITS), F32),
            pltpu.VMEM((2, 3, HALF, UNITS), F32),
            pltpu.VMEM((DEPTH, 3, SEG, CA), BF16),
            pltpu.VMEM((DEPTH, 3, SEG, OA), BF16),
            pltpu.VMEM((DEPTH, 3, SEG, KA), BF16),
            pltpu.VMEM((DEPTH, 2, 3, SEG, CA), BF16),
            pltpu.VMEM((DEPTH, 2, 3, SEG, CA), BF16),
            pltpu.VMEM((DEPTH, 3, SEG, OA), BF16),
            pltpu.VMEM((DEPTH, 3, SEG, OA), BF16),
            pltpu.VMEM((DEPTH, 3, HALF, OB), BF16),
            pltpu.VMEM((DEPTH, 3, HALF, OB), BF16),
            pltpu.VMEM((DEPTH, 3, SEG, OB), BF16),
            pltpu.VMEM((DEPTH, 3, SEG, OL), BF16),
            pltpu.VMEM((DEPTH, 3, SEG, OR), BF16),
            pltpu.VMEM((DEPTH, 2, 3, SEG, OB), BF16),
            pltpu.VMEM((DEPTH, 2, 3, SEG, OB), BF16),
            pltpu.VMEM((OWN, ROWS, WIDTH), BF16),
            pltpu.VMEM((OWN, ROWS, WIDTH), BF16),
            pltpu.VMEM((ROWS, WIDTH), F32),
            pltpu.VMEM((ROWS, WIDTH), F32),
            pltpu.SemaphoreType.DMA((kinds, SLOTS)),
            pltpu.SemaphoreType.DMA((kinds, SLOTS)),
            pltpu.SemaphoreType.DMA((SLOTS,)),
            pltpu.SemaphoreType.DMA((SLOTS,)),
            pltpu.SemaphoreType.DMA((3,)),
            pltpu.SemaphoreType.DMA((3,)),
        ],
        compiler_params=pltpu.CompilerParams(
            collective_id=0, has_side_effects=True, vmem_limit_bytes=30 * 2**20
        ),
        cost_estimate=pl.CostEstimate(
            flops=8 * total * WIDTH * UNITS, bytes_accessed=24 * 2**20, transcendentals=0
        ),
    )(ids, tokens, grad_out, wg, wu, wd)


GRAD_COLUMNS = 640


def grads_kernel(
    mown, gat, tokt, hidt, hh, early,
    mixed, grad_gate, grad_up, grad_down,
    mbuf, gbuf, ubuf, dbuf, sems, msem,
):
    mbuf[...] = mown[...].astype(BF16)
    mcopy = pltpu.make_async_copy(mbuf, mixed, msem)
    mcopy.start()
    total = SLOTS * ROWS
    sc = gat[:, :, WIDTH:].reshape(total, WIDTH)
    blocks = []
    for n in range(UNITS // GRAD_COLUMNS):
        cols = pl.ds(n * GRAD_COLUMNS, GRAD_COLUMNS)
        slot = n % 2
        copies = [
            pltpu.make_async_copy(gbuf.at[slot], grad_gate.at[:, cols], sems.at[0, slot]),
            pltpu.make_async_copy(ubuf.at[slot], grad_up.at[:, cols], sems.at[1, slot]),
            pltpu.make_async_copy(dbuf.at[slot], grad_down.at[cols, :], sems.at[2, slot]),
        ]
        blocks.append(copies)
        for k, buf in enumerate((gbuf, ubuf, dbuf)):
            if n >= 2:
                blocks[n - 2][k].wait()
            if k < 2:
                first = EARLY if k < len(EARLY_STEPS) else 0
                depth = total - first * ROWS
                right = hh[first:, k + 1, :, cols].reshape(depth, GRAD_COLUMNS)
                part = jnp.dot(tokt[:, first * ROWS :], right, preferred_element_type=F32)
                buf[slot] = part + early[k, :, cols] if first else part
            else:
                buf[slot] = jnp.dot(hidt[cols, :], sc, preferred_element_type=F32)
            copies[k].start()
    for copies in blocks[-2:]:
        for copy in copies:
            copy.wait()
    mcopy.wait()


def grads(*arrays):
    total = SLOTS * ROWS
    vmem = pl.BlockSpec(memory_space=pltpu.VMEM)
    hbm = pl.BlockSpec(memory_space=pl.ANY)
    return pl.pallas_call(
        grads_kernel,
        name="grads",
        out_shape=(
            jax.ShapeDtypeStruct((ROWS, WIDTH), BF16),
            jax.ShapeDtypeStruct((WIDTH, UNITS), F32),
            jax.ShapeDtypeStruct((WIDTH, UNITS), F32),
            jax.ShapeDtypeStruct((UNITS, WIDTH), F32),
        ),
        in_specs=[vmem] * 6,
        out_specs=(hbm,) * 4,
        scratch_shapes=[
            pltpu.VMEM((ROWS, WIDTH), BF16),
            pltpu.VMEM((2, WIDTH, GRAD_COLUMNS), F32),
            pltpu.VMEM((2, WIDTH, GRAD_COLUMNS), F32),
            pltpu.VMEM((2, GRAD_COLUMNS, WIDTH), F32),
            pltpu.SemaphoreType.DMA((3, 2)),
            pltpu.SemaphoreType.DMA,
        ],
        compiler_params=pltpu.CompilerParams(vmem_limit_bytes=12 * 2**20),
        cost_estimate=pl.CostEstimate(
            flops=6 * total * WIDTH * UNITS, bytes_accessed=12 * 2**20, transcendentals=0
        ),
    )(*arrays)


def shards(tokens, segment_ids, gate_weight, up_weight, down_weight, grad_out):
    ids = segment_ids.reshape(SLOTS, ROWS)
    arrays = (ids, tokens, grad_out, gate_weight, up_weight, down_weight)
    outs = exchange(*(pltpu.with_memory_space_constraint(a, pltpu.HBM) for a in arrays))
    return grads(*outs)


def solution(mesh):
    placed = (
        P("tensor", "dp"),
        P(),
        P("dp", "tensor"),
        P("dp", "tensor"),
        P("tensor", "dp"),
        P("tensor", "dp"),
    )
    return jax.shard_map(
        shards,
        mesh=mesh,
        in_specs=placed,
        out_specs=(P("tensor", "dp"), P("dp", "tensor"), P("dp", "tensor"), P("tensor", "dp")),
        check_vma=False,
    )
```

```python
import jax
import jax.numpy as jnp
from jax import lax
from jax.experimental import pallas as pl
from jax.experimental.pallas import tpu as pltpu
from jax.sharding import PartitionSpec as P

NSEG = 8
SLOTS = 8
ROWS = 128
HALF = 64
SEG = 16
OWN, MATE = 7, 1
WIDTH = 512
UNITS = 1920
TILE = 128
MESH = pl.DeviceIdType.MESH
BF16 = jnp.bfloat16
F32 = jnp.float32
DOT_COLUMNS = ((0, 512), (512, 512), (1024, 512), (1536, 384))

JOIN = 18
EARLY = 4
EARLY_STEPS = (17, 18)

CA = 1152
CB = UNITS - CA
OA = -(-CA // (2 * TILE)) * TILE
KA = CA - OA
OB = -(-CB // (2 * TILE)) * TILE
KB = CB - OB
OL = OB // (2 * TILE) * TILE
OR = OB - OL

DEPTH = 4
NAMES = (
    "core0", "core1", "core2", "x1p", "x1m", "x2p", "x2m", "zred", "zgat", "g1p", "g1m", "g2p", "g2m", "cgat",
    "mix", "y0", "y1p", "y1m", "y2p", "y2m", "k1p", "k1m", "k2p", "k2m", "k3",
)
KIND = {name: i for i, name in enumerate(NAMES)}


def exchange_kernel(
    ids_hbm, tokens_hbm, grad_out_hbm, wg_hbm, wu_hbm, wd_hbm,
    mown, gat, tokt, hidt, hh, early,
    ids, grad_out, wg, wu, wd, acc, cs, cr, x1s, x1a, x1b, x2s, x2r, zs, zr,
    y0s, y0r, y1s, y1a, y1b, y2s, y2r, ms, mr, mfr, mfar,
    ss, rs, ts, tr, ws, own_sems,
):
    inputs = [
        pltpu.make_async_copy(a, b, own_sems.at[k])
        for k, (a, b) in enumerate(
            ((ids_hbm, ids), (grad_out_hbm, grad_out), (tokens_hbm, gat.at[OWN, :, :WIDTH]))
        )
    ]
    for copy in inputs:
        copy.start()
    weights = [
        pltpu.make_async_copy(a, b, ws.at[k])
        for k, (a, b) in enumerate(((wg_hbm, wg), (wu_hbm, wu), (wd_hbm, wd)))
    ]
    for copy in weights:
        copy.start()

    dp = lax.axis_index("dp")
    tn = lax.axis_index("tensor")
    w, x, q = dp // 8, (dp // 2) % 4, dp % 2
    y, h = tn // 2, tn % 2
    xp, xm, xo = (x + 1) % 4, (x + 3) % 4, (x + 2) % 4

    def dpdev(w=w, x=x, q=q):
        return (w * 8 + x * 2 + q, tn)

    def tdev(dy, dh):
        return (dp, ((y + dy) % 4) * 2 + (h + dh) % 2)

    core, right, left, zmate = dpdev(q=1 - q), dpdev(x=xp), dpdev(x=xm), dpdev(w=1 - w)
    offsets = [(1, 0), (0, 1), (1, 1), (3, 1), (2, 1), (3, 0), (2, 0), (0, 0)]

    barrier = pltpu.get_barrier_semaphore()
    partners = [core, right, left, zmate] + [tdev(*o) for o in offsets[:OWN]]
    for p in partners:
        pl.semaphore_signal(barrier, inc=1, device_id=p, device_id_type=MESH)

    for copy in inputs:
        copy.wait()
    all_ids = ids[...]
    own_ids = ids[pl.ds(tn, 1), :]
    row = jnp.zeros((1, ROWS), F32)
    for s in range(NSEG):
        length = jnp.sum(jnp.where(all_ids == s, 1.0, 0.0), axis=(0, 1), keepdims=True)
        row = jnp.where(own_ids == s, lax.rsqrt(length), row)
    square = jnp.broadcast_to(row, (ROWS, ROWS))
    on_diagonal = lax.broadcasted_iota(jnp.int32, (ROWS, ROWS), 0) == lax.broadcasted_iota(
        jnp.int32, (ROWS, ROWS), 1
    )
    column = jnp.sum(jnp.where(on_diagonal, square, 0.0), axis=1, keepdims=True)
    gat[OWN, :, WIDTH:] = (grad_out[...].astype(F32) * column).astype(BF16)

    pl.semaphore_wait(barrier, len(partners))

    def rows_of(xx):
        return pl.ds(pl.multiple_of(q * HALF + xx * SEG, SEG), SEG)

    def seg_of(xx):
        return pl.ds(pl.multiple_of(xx * SEG, SEG), SEG)

    def half_of(qq):
        return pl.ds(pl.multiple_of(qq * HALF, HALF), HALF)

    def cols_of(start, size):
        return pl.ds(pl.multiple_of(start, TILE), size)

    def msg(name, c, src, dst, dev):
        kind = KIND[name]
        return pltpu.make_async_remote_copy(
            src_ref=src, dst_ref=dst, send_sem=ss.at[kind, c], recv_sem=rs.at[kind, c],
            device_id=dev, device_id_type=MESH,
        )

    def tok_msg(slot, src, dev):
        return pltpu.make_async_remote_copy(
            src_ref=src, dst_ref=gat.at[slot], send_sem=ts.at[slot], recv_sem=tr.at[slot],
            device_id=dev, device_id_type=MESH,
        )

    def in_place(name, c, rows, cols, dev):
        ref = hh.at[c, :, rows, cols]
        return msg(name, c, ref, ref, dev)

    own_a, mate_a = cols_of(w * KA, OA), cols_of((1 - w) * KA, OA)
    out_a, in_a = cols_of(w * OA, KA), cols_of((1 - w) * OA, KA)
    own_b, mate_b = cols_of(CA + w * KB, OB), cols_of(CA + (1 - w) * KB, OB)
    own_b_left = cols_of(CA + w * KB, OL)
    own_b_right = cols_of(CA + w * KB + OL, OR)
    out_b, in_b = cols_of(CA + w * OB, KB), cols_of(CA + (1 - w) * OB, KB)
    all_a, lo_a, hi_a = pl.ds(0, CA), pl.ds(0, OA), pl.ds(OA, KA)

    def m_core(c, k):
        return msg(f"core{k}", c, cs.at[c % 2, k], cr.at[c % 2, k], core)

    def m_x1p(c):
        return msg("x1p", c, x1s.at[c % DEPTH, :, :, lo_a], x1a.at[c % DEPTH], right)

    def m_x1m(c):
        return msg("x1m", c, x1s.at[c % DEPTH, :, :, hi_a], x1b.at[c % DEPTH], left)

    def m_x2p(c):
        return msg("x2p", c, x2s.at[c % DEPTH, 0], x2r.at[c % DEPTH, 0], right)

    def m_x2m(c):
        return msg("x2m", c, x2s.at[c % DEPTH, 1], x2r.at[c % DEPTH, 1], left)

    def m_zred(c):
        return msg("zred", c, zs.at[c % DEPTH], zr.at[c % DEPTH], zmate)

    def m_zgat(c, cols):
        return in_place("zgat", c, rows_of(x), cols, zmate)

    def m_g1p(c, xx):
        return in_place("g1p", c, rows_of(xx), all_a, right)

    def m_g1m(c, xx):
        return in_place("g1m", c, rows_of(xx), all_a, left)

    def m_g2p(c, xx):
        return in_place("g2p", c, rows_of(xx), hi_a, right)

    def m_g2m(c, xx):
        return in_place("g2m", c, rows_of(xx), lo_a, left)

    def m_y0(c):
        return msg("y0", c, y0s.at[c % DEPTH], y0r.at[c % DEPTH], zmate)

    def m_y1p(c):
        return msg("y1p", c, y1s.at[c % DEPTH, :, :, :OL], y1a.at[c % DEPTH], right)

    def m_y1m(c):
        return msg("y1m", c, y1s.at[c % DEPTH, :, :, OL:], y1b.at[c % DEPTH], left)

    def m_y2p(c):
        return msg("y2p", c, y2s.at[c % DEPTH, 0], y2r.at[c % DEPTH, 0], right)

    def m_y2m(c):
        return msg("y2m", c, y2s.at[c % DEPTH, 1], y2r.at[c % DEPTH, 1], left)

    def m_k1p(c, xx):
        return in_place("k1p", c, rows_of(xx), own_b, right)

    def m_k1m(c, xx):
        return in_place("k1m", c, rows_of(xx), own_b, left)

    def m_k2p(c, xx):
        return in_place("k2p", c, rows_of(xx), own_b_right, right)

    def m_k2m(c, xx):
        return in_place("k2m", c, rows_of(xx), own_b_left, left)

    def m_k3(c, cols):
        return in_place("k3", c, half_of(q), cols, zmate)

    def m_cgat(c, qq):
        ref = hh.at[c, :, half_of(qq), :]
        return msg("cgat", c, ref, ref, core)

    def m_mix(c):
        dy = jnp.where(c == 0, 1, jnp.where(c % 2 == 1, 3, jnp.where(c == 2, 1, 2)))
        return msg("mix", c, ms.at[c], mr.at[c], tdev(dy, 0))

    def m_far():
        return msg("mix", OWN, mfar, mfr, tdev(0, 1))

    for s in (0, 5, MATE):
        dy, dh = offsets[s]
        tok_msg(s, gat.at[OWN], tdev(-dy % 4, dh)).start()
    for copy in weights:
        copy.wait()

    def a_partials(c, r):
        @pl.when((c != OWN) & (c != MATE))
        def _():
            tok_msg(c, gat.at[OWN], core).wait_recv()

        both = jnp.concatenate([gat[c, half_of(1 - q), :], gat[c, half_of(q), :]], axis=0)
        tok, sc = both[:, :WIDTH], both[:, WIDTH:]
        for k, mat in enumerate((wg, wu, wd)):
            for n0, nw in DOT_COLUMNS:
                cols = slice(n0, n0 + nw)
                if k < 2:
                    part = jnp.dot(tok, mat[:, cols], preferred_element_type=F32)
                else:
                    part = lax.dot_general(
                        sc, mat[cols, :], (((1,), (1,)), ((), ())), preferred_element_type=F32
                    )
                cs[r % 2, k, :, cols] = part[:HALF]
                acc[r % 5, k, :, cols] = part[HALF:]
            m_core(r, k).start()

    def forward_tokens():
        tok_msg(MATE, gat.at[OWN], core).wait_recv()
        for s in (2, 3):
            tok_msg(s, gat.at[MATE], tdev(-offsets[s][0] % 4, 0)).start()

    def send_far_tokens():
        tok_msg(4, gat.at[MATE], tdev(2, 0)).start()
        tok_msg(6, gat.at[OWN], tdev(2, 0)).start()

    def b_stage(c, r):
        a = r % 5
        for k in range(3):
            m_core(r, k).wait_recv()
        acc[a] += cr[r % 2]
        x1s[r % DEPTH] = acc[a, :, seg_of(xo), :CA].astype(BF16)
        m_x1p(r).start()
        m_x1m(r).start()
        y0s[r % DEPTH] = acc[a, :, :, mate_b].astype(BF16)
        m_y0(r).start()
        for k in range(3):
            m_core(r, k).wait_send()

    def c_stage(c, r):
        a = r % 5
        m_x1p(r).wait_recv()
        m_x1m(r).wait_recv()
        acc[a, :, seg_of(xp), :OA] += x1a[r % DEPTH].astype(F32)
        acc[a, :, seg_of(xm), OA:CA] += x1b[r % DEPTH].astype(F32)
        x2s[r % DEPTH, 0] = acc[a, :, seg_of(xp), :CA].astype(BF16)
        x2s[r % DEPTH, 1] = acc[a, :, seg_of(xm), :CA].astype(BF16)
        m_x2p(r).start()
        m_x2m(r).start()

    def c2_stage(c, r):
        a = r % 5
        m_y0(r).wait_recv()
        acc[a, :, :, own_b] += y0r[r % DEPTH].astype(F32)
        y1s[r % DEPTH] = acc[a, :, seg_of(xo), own_b].astype(BF16)
        m_y1p(r).start()
        m_y1m(r).start()

    def d_stage(c, r):
        a = r % 5
        m_x2p(r).wait_recv()
        m_x2m(r).wait_recv()
        acc[a, :, seg_of(x), :CA] += x2r[r % DEPTH, 0].astype(F32) + x2r[r % DEPTH, 1].astype(F32)
        zs[r % DEPTH] = acc[a, :, seg_of(x), mate_a].astype(BF16)
        m_zred(r).start()

    def d2_stage(c, r):
        a = r % 5
        m_y1p(r).wait_recv()
        m_y1m(r).wait_recv()
        acc[a, :, seg_of(xp), own_b_left] += y1a[r % DEPTH].astype(F32)
        acc[a, :, seg_of(xm), own_b_right] += y1b[r % DEPTH].astype(F32)
        y2s[r % DEPTH, 0] = acc[a, :, seg_of(xp), own_b].astype(BF16)
        y2s[r % DEPTH, 1] = acc[a, :, seg_of(xm), own_b].astype(BF16)
        m_y2p(r).start()
        m_y2m(r).start()

    def finish_units(c, tot, cols):
        gate, up, dhid = tot[0], tot[1], tot[2]
        sig = jax.nn.sigmoid(gate)
        hh[c, 0, rows_of(x), cols] = (gate * sig * up).astype(BF16)
        hh[c, 1, rows_of(x), cols] = (dhid * up * sig * (1.0 + gate * (1.0 - sig))).astype(BF16)
        hh[c, 2, rows_of(x), cols] = (dhid * gate * sig).astype(BF16)

    def e_stage(c, r):
        a = r % 5
        for message in (m_x1p(r), m_x1m(r), m_x2p(r), m_x2m(r), m_zred(r)):
            message.wait_send()
        m_zred(r).wait_recv()
        finish_units(c, acc[a, :, seg_of(x), own_a] + zr[r % DEPTH].astype(F32), own_a)
        m_zgat(c, out_a).start()

    def e2_stage(c, r):
        a = r % 5
        for message in (m_y0(r), m_y1p(r), m_y1m(r), m_y2p(r), m_y2m(r)):
            message.wait_send()
        m_y2p(r).wait_recv()
        m_y2m(r).wait_recv()
        tot = acc[a, :, seg_of(x), own_b] + y2r[r % DEPTH, 0].astype(F32) + y2r[r % DEPTH, 1].astype(F32)
        finish_units(c, tot, own_b)
        m_k1p(c, x).start()
        m_k1m(c, x).start()

    def f_stage(c):
        m_zgat(c, in_a).wait_recv()
        m_g1p(c, x).start()
        m_g1m(c, x).start()

    def f2_stage(c):
        m_k1p(c, xm).wait_recv()
        m_k2p(c, xm).start()
        m_k1m(c, xp).wait_recv()
        m_k2m(c, xp).start()

    def g_stage(c):
        m_g1p(c, xm).wait_recv()
        m_g2p(c, xm).start()
        m_g1m(c, xp).wait_recv()
        m_g2m(c, xp).start()

    def g2_stage(c):
        m_k2p(c, xo).wait_recv()
        m_k2m(c, xo).wait_recv()
        m_k3(c, out_b).start()

    def h_stage(c):
        m_g2p(c, xo).wait_recv()
        m_g2m(c, xo).wait_recv()
        m_k3(c, in_b).wait_recv()
        m_cgat(c, q).start()

    def i_stage(c):
        m_cgat(c, 1 - q).wait_recv()
        part = jnp.dot(hh[c, 0], wd[...], preferred_element_type=F32)

        @pl.when(c == OWN)
        def _():
            mown[...] = part

        @pl.when(c == MATE)
        def _():
            mfar[...] = part

        @pl.when((c != OWN) & (c != MATE))
        def _():
            ms[c] = part.astype(BF16)
            m_mix(c).start()

        tokens_c = cols_of(c * ROWS, ROWS)
        hidt[:, tokens_c] = hh[c, 0].T
        tokt[:, tokens_c] = gat[c, :, :WIDTH].T

    def join_mixed():
        for c in (2, 3, 4):
            m_mix(c).wait_recv()
            mfar[...] += mr[c].astype(F32)
        m_far().start()

    def early_gradient(k):
        depth = EARLY * ROWS
        for n0, nw in DOT_COLUMNS:
            block = pl.ds(n0, nw)
            right = hh[:EARLY, k + 1, :, block].reshape(depth, nw)
            early[k, :, block] = jnp.dot(tokt[:, :depth], right, preferred_element_type=F32)

    plan = [
        (e_stage, 5, False), (c_stage, 2, False), (g2_stage, 9, True), (g_stage, 11, True),
        (f_stage, 9, True), (b_stage, 1, False), (d_stage, 3, False), (f2_stage, 7, True),
        (a_partials, 0, False), (h_stage, 12, True), (e2_stage, 4, False), (c2_stage, 2, False),
        (d2_stage, 3, False), (i_stage, 13, True),
    ]
    last = max(lag for _, lag, _ in plan)

    def step(i, carry):
        for stage, lag, back in plan:
            j = i - lag
            @pl.when((j >= 0) & (j < SLOTS))
            def _(stage=stage, j=j, back=back):
                if back:
                    stage(j)
                else:
                    slot = jnp.where(j == 0, OWN, jnp.where(j == 1, 0, jnp.where(j == 2, 5, j - 2)))
                    stage(jnp.where(j == 7, 6, slot), j)

        @pl.when(i == 1)
        def _():
            forward_tokens()

        @pl.when(i == 2)
        def _():
            send_far_tokens()

        @pl.when(i == JOIN)
        def _():
            join_mixed()

        for k, at in enumerate(EARLY_STEPS):

            @pl.when(i == at)
            def _(k=k):
                early_gradient(k)

        return carry

    lax.fori_loop(0, SLOTS + last, step, 0)

    for c in (0, 5, 6):
        m_mix(c).wait_recv()
        mown[...] += mr[c].astype(F32)
    m_far().wait_recv()
    mown[...] += mfr[...]

    def drain(c, carry):
        for message in (
            m_zgat(c, out_a), m_g1p(c, x), m_g1m(c, x), m_g2p(c, xm), m_g2m(c, xp),
            m_cgat(c, q), m_k1p(c, x), m_k1m(c, x), m_k2p(c, xm), m_k2m(c, xp), m_k3(c, out_b),
        ):
            message.wait_send()

        @pl.when((c != OWN) & (c != MATE))
        def _():
            m_mix(c).wait_send()

        @pl.when(c != OWN)
        def _():
            tok_msg(c, gat.at[OWN], core).wait_send()

        return carry

    lax.fori_loop(0, SLOTS, drain, 0)
    m_far().wait_send()


def exchange(ids, tokens, grad_out, wg, wu, wd):
    vmem = pl.BlockSpec(memory_space=pltpu.VMEM)
    hbm = pl.BlockSpec(memory_space=pltpu.HBM)
    total = SLOTS * ROWS
    kinds = len(NAMES)
    return pl.pallas_call(
        exchange_kernel,
        name="exchange",
        out_shape=(
            pltpu.VMEM((ROWS, WIDTH), F32),
            pltpu.VMEM((SLOTS, ROWS, 2 * WIDTH), BF16),
            pltpu.VMEM((WIDTH, total), BF16),
            pltpu.VMEM((UNITS, total), BF16),
            pltpu.VMEM((SLOTS, 3, ROWS, UNITS), BF16),
            pltpu.VMEM((len(EARLY_STEPS), WIDTH, UNITS), F32),
        ),
        in_specs=[hbm] * 6,
        out_specs=(vmem,) * 6,
        scratch_shapes=[
            pltpu.VMEM((SLOTS, ROWS), jnp.int32),
            pltpu.VMEM((ROWS, WIDTH), BF16),
            pltpu.VMEM((WIDTH, UNITS), BF16),
            pltpu.VMEM((WIDTH, UNITS), BF16),
            pltpu.VMEM((UNITS, WIDTH), BF16),
            pltpu.VMEM((5, 3, HALF, UNITS), F32),
            pltpu.VMEM((2, 3, HALF, UNITS), F32),
            pltpu.VMEM((2, 3, HALF, UNITS), F32),
            pltpu.VMEM((DEPTH, 3, SEG, CA), BF16),
            pltpu.VMEM((DEPTH, 3, SEG, OA), BF16),
            pltpu.VMEM((DEPTH, 3, SEG, KA), BF16),
            pltpu.VMEM((DEPTH, 2, 3, SEG, CA), BF16),
            pltpu.VMEM((DEPTH, 2, 3, SEG, CA), BF16),
            pltpu.VMEM((DEPTH, 3, SEG, OA), BF16),
            pltpu.VMEM((DEPTH, 3, SEG, OA), BF16),
            pltpu.VMEM((DEPTH, 3, HALF, OB), BF16),
            pltpu.VMEM((DEPTH, 3, HALF, OB), BF16),
            pltpu.VMEM((DEPTH, 3, SEG, OB), BF16),
            pltpu.VMEM((DEPTH, 3, SEG, OL), BF16),
            pltpu.VMEM((DEPTH, 3, SEG, OR), BF16),
            pltpu.VMEM((DEPTH, 2, 3, SEG, OB), BF16),
            pltpu.VMEM((DEPTH, 2, 3, SEG, OB), BF16),
            pltpu.VMEM((OWN, ROWS, WIDTH), BF16),
            pltpu.VMEM((OWN, ROWS, WIDTH), BF16),
            pltpu.VMEM((ROWS, WIDTH), F32),
            pltpu.VMEM((ROWS, WIDTH), F32),
            pltpu.SemaphoreType.DMA((kinds, SLOTS)),
            pltpu.SemaphoreType.DMA((kinds, SLOTS)),
            pltpu.SemaphoreType.DMA((SLOTS,)),
            pltpu.SemaphoreType.DMA((SLOTS,)),
            pltpu.SemaphoreType.DMA((3,)),
            pltpu.SemaphoreType.DMA((3,)),
        ],
        compiler_params=pltpu.CompilerParams(
            collective_id=0, has_side_effects=True, vmem_limit_bytes=30 * 2**20
        ),
        cost_estimate=pl.CostEstimate(
            flops=8 * total * WIDTH * UNITS, bytes_accessed=24 * 2**20, transcendentals=0
        ),
    )(ids, tokens, grad_out, wg, wu, wd)


GRAD_COLUMNS = 640


def grads_kernel(
    mown, gat, tokt, hidt, hh, early,
    mixed, grad_gate, grad_up, grad_down,
    mbuf, gbuf, ubuf, dbuf, sems, msem,
):
    mbuf[...] = mown[...].astype(BF16)
    mcopy = pltpu.make_async_copy(mbuf, mixed, msem)
    mcopy.start()
    total = SLOTS * ROWS
    sc = gat[:, :, WIDTH:].reshape(total, WIDTH)
    blocks = []
    for n in range(UNITS // GRAD_COLUMNS):
        cols = pl.ds(n * GRAD_COLUMNS, GRAD_COLUMNS)
        slot = n % 2
        copies = [
            pltpu.make_async_copy(gbuf.at[slot], grad_gate.at[:, cols], sems.at[0, slot]),
            pltpu.make_async_copy(ubuf.at[slot], grad_up.at[:, cols], sems.at[1, slot]),
            pltpu.make_async_copy(dbuf.at[slot], grad_down.at[cols, :], sems.at[2, slot]),
        ]
        blocks.append(copies)
        for k, buf in enumerate((gbuf, ubuf, dbuf)):
            if n >= 2:
                blocks[n - 2][k].wait()
            if k < 2:
                first = EARLY if k < len(EARLY_STEPS) else 0
                depth = total - first * ROWS
                right = hh[first:, k + 1, :, cols].reshape(depth, GRAD_COLUMNS)
                part = jnp.dot(tokt[:, first * ROWS :], right, preferred_element_type=F32)
                buf[slot] = part + early[k, :, cols] if first else part
            else:
                buf[slot] = jnp.dot(hidt[cols, :], sc, preferred_element_type=F32)
            copies[k].start()
    for copies in blocks[-2:]:
        for copy in copies:
            copy.wait()
    mcopy.wait()


def grads(*arrays):
    total = SLOTS * ROWS
    vmem = pl.BlockSpec(memory_space=pltpu.VMEM)
    hbm = pl.BlockSpec(memory_space=pl.ANY)
    return pl.pallas_call(
        grads_kernel,
        name="grads",
        out_shape=(
            jax.ShapeDtypeStruct((ROWS, WIDTH), BF16),
            jax.ShapeDtypeStruct((WIDTH, UNITS), F32),
            jax.ShapeDtypeStruct((WIDTH, UNITS), F32),
            jax.ShapeDtypeStruct((UNITS, WIDTH), F32),
        ),
        in_specs=[vmem] * 6,
        out_specs=(hbm,) * 4,
        scratch_shapes=[
            pltpu.VMEM((ROWS, WIDTH), BF16),
            pltpu.VMEM((2, WIDTH, GRAD_COLUMNS), F32),
            pltpu.VMEM((2, WIDTH, GRAD_COLUMNS), F32),
            pltpu.VMEM((2, GRAD_COLUMNS, WIDTH), F32),
            pltpu.SemaphoreType.DMA((3, 2)),
            pltpu.SemaphoreType.DMA,
        ],
        compiler_params=pltpu.CompilerParams(vmem_limit_bytes=9 * 2**20),
        cost_estimate=pl.CostEstimate(
            flops=6 * total * WIDTH * UNITS, bytes_accessed=12 * 2**20, transcendentals=0
        ),
    )(*arrays)


def shards(tokens, segment_ids, gate_weight, up_weight, down_weight, grad_out):
    ids = segment_ids.reshape(SLOTS, ROWS)
    arrays = (ids, tokens, grad_out, gate_weight, up_weight, down_weight)
    outs = exchange(*(pltpu.with_memory_space_constraint(a, pltpu.HBM) for a in arrays))
    return grads(*outs)


def solution(mesh):
    placed = (
        P("tensor", "dp"),
        P(),
        P("dp", "tensor"),
        P("dp", "tensor"),
        P("tensor", "dp"),
        P("tensor", "dp"),
    )
    return jax.shard_map(
        shards,
        mesh=mesh,
        in_specs=placed,
        out_specs=(P("tensor", "dp"), P("dp", "tensor"), P("dp", "tensor"), P("tensor", "dp")),
        check_vma=False,
    )
```

```python
import jax
import jax.numpy as jnp
from jax import lax
from jax.experimental import pallas as pl
from jax.experimental.pallas import tpu as pltpu
from jax.sharding import PartitionSpec as P

NSEG = 8
SLOTS = 8
ROWS = 128
HALF = 64
SEG = 16
OWN, MATE = 7, 1
WIDTH = 512
UNITS = 1920
TILE = 128
MESH = pl.DeviceIdType.MESH
BF16 = jnp.bfloat16
F32 = jnp.float32
DOT_COLUMNS = ((0, 512), (512, 512), (1024, 512), (1536, 384))

JOIN = 18
EARLY = 4
EARLY_STEPS = (17, 18)

CA = 1152
CB = UNITS - CA
OA = -(-CA // (2 * TILE)) * TILE
KA = CA - OA
OB = -(-CB // (2 * TILE)) * TILE
KB = CB - OB
OL = OB // (2 * TILE) * TILE
OR = OB - OL

DEPTH = 4
NAMES = (
    "core0", "core1", "core2", "x1p", "x1m", "x2p", "x2m", "zred", "zgat", "g1p", "g1m", "g2p", "g2m", "cgat",
    "mix", "y0", "y1p", "y1m", "y2p", "y2m", "k1p", "k1m", "k2p", "k2m", "k3",
)
KIND = {name: i for i, name in enumerate(NAMES)}


def exchange_kernel(
    ids_hbm, tokens_hbm, grad_out_hbm, wg_hbm, wu_hbm, wd_hbm,
    mown, gat, tokt, hidt, hh, early,
    ids, grad_out, wg, wu, wd, acc, cs, cr, x1s, x1a, x1b, x2s, x2r, zs, zr,
    y0s, y0r, y1s, y1a, y1b, y2s, y2r, ms, mr, mfr, mfar,
    ss, rs, ts, tr, ws, own_sems,
):
    inputs = [
        pltpu.make_async_copy(a, b, own_sems.at[k])
        for k, (a, b) in enumerate(
            ((ids_hbm, ids), (grad_out_hbm, grad_out), (tokens_hbm, gat.at[OWN, :, :WIDTH]))
        )
    ]
    for copy in inputs:
        copy.start()
    weights = [
        pltpu.make_async_copy(a, b, ws.at[k])
        for k, (a, b) in enumerate(((wg_hbm, wg), (wu_hbm, wu), (wd_hbm, wd)))
    ]
    for copy in weights:
        copy.start()

    dp = lax.axis_index("dp")
    tn = lax.axis_index("tensor")
    w, x, q = dp // 8, (dp // 2) % 4, dp % 2
    y, h = tn // 2, tn % 2
    xp, xm, xo = (x + 1) % 4, (x + 3) % 4, (x + 2) % 4

    def dpdev(w=w, x=x, q=q):
        return (w * 8 + x * 2 + q, tn)

    def tdev(dy, dh):
        return (dp, ((y + dy) % 4) * 2 + (h + dh) % 2)

    core, right, left, zmate = dpdev(q=1 - q), dpdev(x=xp), dpdev(x=xm), dpdev(w=1 - w)
    offsets = [(1, 0), (0, 1), (1, 1), (3, 1), (2, 1), (3, 0), (2, 0), (0, 0)]

    barrier = pltpu.get_barrier_semaphore()
    partners = [core, right, left, zmate] + [tdev(*o) for o in offsets[:OWN]]
    for p in partners:
        pl.semaphore_signal(barrier, inc=1, device_id=p, device_id_type=MESH)

    for copy in inputs:
        copy.wait()
    all_ids = ids[...]
    own_ids = ids[pl.ds(tn, 1), :]
    row = jnp.zeros((1, ROWS), F32)
    for s in range(NSEG):
        length = jnp.sum(jnp.where(all_ids == s, 1.0, 0.0), axis=(0, 1), keepdims=True)
        row = jnp.where(own_ids == s, lax.rsqrt(length), row)
    square = jnp.broadcast_to(row, (ROWS, ROWS))
    on_diagonal = lax.broadcasted_iota(jnp.int32, (ROWS, ROWS), 0) == lax.broadcasted_iota(
        jnp.int32, (ROWS, ROWS), 1
    )
    column = jnp.sum(jnp.where(on_diagonal, square, 0.0), axis=1, keepdims=True)
    gat[OWN, :, WIDTH:] = (grad_out[...].astype(F32) * column).astype(BF16)

    pl.semaphore_wait(barrier, len(partners))

    def rows_of(xx):
        return pl.ds(pl.multiple_of(q * HALF + xx * SEG, SEG), SEG)

    def seg_of(xx):
        return pl.ds(pl.multiple_of(xx * SEG, SEG), SEG)

    def half_of(qq):
        return pl.ds(pl.multiple_of(qq * HALF, HALF), HALF)

    def cols_of(start, size):
        return pl.ds(pl.multiple_of(start, TILE), size)

    def msg(name, c, src, dst, dev):
        kind = KIND[name]
        return pltpu.make_async_remote_copy(
            src_ref=src, dst_ref=dst, send_sem=ss.at[kind, c], recv_sem=rs.at[kind, c],
            device_id=dev, device_id_type=MESH,
        )

    def tok_msg(slot, src, dev):
        return pltpu.make_async_remote_copy(
            src_ref=src, dst_ref=gat.at[slot], send_sem=ts.at[slot], recv_sem=tr.at[slot],
            device_id=dev, device_id_type=MESH,
        )

    def in_place(name, c, rows, cols, dev):
        ref = hh.at[c, :, rows, cols]
        return msg(name, c, ref, ref, dev)

    own_a, mate_a = cols_of(w * KA, OA), cols_of((1 - w) * KA, OA)
    out_a, in_a = cols_of(w * OA, KA), cols_of((1 - w) * OA, KA)
    own_b, mate_b = cols_of(CA + w * KB, OB), cols_of(CA + (1 - w) * KB, OB)
    own_b_left = cols_of(CA + w * KB, OL)
    own_b_right = cols_of(CA + w * KB + OL, OR)
    out_b, in_b = cols_of(CA + w * OB, KB), cols_of(CA + (1 - w) * OB, KB)
    all_a, lo_a, hi_a = pl.ds(0, CA), pl.ds(0, OA), pl.ds(OA, KA)

    def m_core(c, k):
        return msg(f"core{k}", c, cs.at[c % 2, k], cr.at[c % 2, k], core)

    def m_x1p(c):
        return msg("x1p", c, x1s.at[c % DEPTH, :, :, lo_a], x1a.at[c % DEPTH], right)

    def m_x1m(c):
        return msg("x1m", c, x1s.at[c % DEPTH, :, :, hi_a], x1b.at[c % DEPTH], left)

    def m_x2p(c):
        return msg("x2p", c, x2s.at[c % DEPTH, 0], x2r.at[c % DEPTH, 0], right)

    def m_x2m(c):
        return msg("x2m", c, x2s.at[c % DEPTH, 1], x2r.at[c % DEPTH, 1], left)

    def m_zred(c):
        return msg("zred", c, zs.at[c % DEPTH], zr.at[c % DEPTH], zmate)

    def m_zgat(c, cols):
        return in_place("zgat", c, rows_of(x), cols, zmate)

    def m_g1p(c, xx):
        return in_place("g1p", c, rows_of(xx), all_a, right)

    def m_g1m(c, xx):
        return in_place("g1m", c, rows_of(xx), all_a, left)

    def m_g2p(c, xx):
        return in_place("g2p", c, rows_of(xx), hi_a, right)

    def m_g2m(c, xx):
        return in_place("g2m", c, rows_of(xx), lo_a, left)

    def m_y0(c):
        return msg("y0", c, y0s.at[c % DEPTH], y0r.at[c % DEPTH], zmate)

    def m_y1p(c):
        return msg("y1p", c, y1s.at[c % DEPTH, :, :, :OL], y1a.at[c % DEPTH], right)

    def m_y1m(c):
        return msg("y1m", c, y1s.at[c % DEPTH, :, :, OL:], y1b.at[c % DEPTH], left)

    def m_y2p(c):
        return msg("y2p", c, y2s.at[c % DEPTH, 0], y2r.at[c % DEPTH, 0], right)

    def m_y2m(c):
        return msg("y2m", c, y2s.at[c % DEPTH, 1], y2r.at[c % DEPTH, 1], left)

    def m_k1p(c, xx):
        return in_place("k1p", c, rows_of(xx), own_b, right)

    def m_k1m(c, xx):
        return in_place("k1m", c, rows_of(xx), own_b, left)

    def m_k2p(c, xx):
        return in_place("k2p", c, rows_of(xx), own_b_right, right)

    def m_k2m(c, xx):
        return in_place("k2m", c, rows_of(xx), own_b_left, left)

    def m_k3(c, cols):
        return in_place("k3", c, half_of(q), cols, zmate)

    def m_cgat(c, qq):
        ref = hh.at[c, :, half_of(qq), :]
        return msg("cgat", c, ref, ref, core)

    def m_mix(c):
        dy = jnp.where(c == 0, 1, jnp.where(c % 2 == 1, 3, jnp.where(c == 2, 1, 2)))
        return msg("mix", c, ms.at[c], mr.at[c], tdev(dy, 0))

    def m_far():
        return msg("mix", OWN, mfar, mfr, tdev(0, 1))

    for s in (0, 5, MATE):
        dy, dh = offsets[s]
        tok_msg(s, gat.at[OWN], tdev(-dy % 4, dh)).start()
    for copy in weights:
        copy.wait()

    def a_partials(c, r):
        @pl.when((c != OWN) & (c != MATE))
        def _():
            tok_msg(c, gat.at[OWN], core).wait_recv()

        both = jnp.concatenate([gat[c, half_of(1 - q), :], gat[c, half_of(q), :]], axis=0)
        tok, sc = both[:, :WIDTH], both[:, WIDTH:]
        for k, mat in enumerate((wg, wu, wd)):
            for n0, nw in DOT_COLUMNS:
                cols = slice(n0, n0 + nw)
                if k < 2:
                    part = jnp.dot(tok, mat[:, cols], preferred_element_type=F32)
                else:
                    part = lax.dot_general(
                        sc, mat[cols, :], (((1,), (1,)), ((), ())), preferred_element_type=F32
                    )
                cs[r % 2, k, :, cols] = part[:HALF]
                acc[r % 5, k, :, cols] = part[HALF:]
            m_core(r, k).start()

    def forward_tokens():
        tok_msg(MATE, gat.at[OWN], core).wait_recv()
        for s in (2, 3):
            tok_msg(s, gat.at[MATE], tdev(-offsets[s][0] % 4, 0)).start()

    def send_far_tokens():
        tok_msg(4, gat.at[MATE], tdev(2, 0)).start()
        tok_msg(6, gat.at[OWN], tdev(2, 0)).start()

    def b_stage(c, r):
        a = r % 5
        for k in range(3):
            m_core(r, k).wait_recv()
        acc[a] += cr[r % 2]
        x1s[r % DEPTH] = acc[a, :, seg_of(xo), :CA].astype(BF16)
        m_x1p(r).start()
        m_x1m(r).start()
        y0s[r % DEPTH] = acc[a, :, :, mate_b].astype(BF16)
        m_y0(r).start()
        for k in range(3):
            m_core(r, k).wait_send()

    def c_stage(c, r):
        a = r % 5
        m_x1p(r).wait_recv()
        m_x1m(r).wait_recv()
        acc[a, :, seg_of(xp), :OA] += x1a[r % DEPTH].astype(F32)
        acc[a, :, seg_of(xm), OA:CA] += x1b[r % DEPTH].astype(F32)
        x2s[r % DEPTH, 0] = acc[a, :, seg_of(xp), :CA].astype(BF16)
        x2s[r % DEPTH, 1] = acc[a, :, seg_of(xm), :CA].astype(BF16)
        m_x2p(r).start()
        m_x2m(r).start()

    def c2_stage(c, r):
        a = r % 5
        m_y0(r).wait_recv()
        acc[a, :, :, own_b] += y0r[r % DEPTH].astype(F32)
        y1s[r % DEPTH] = acc[a, :, seg_of(xo), own_b].astype(BF16)
        m_y1p(r).start()
        m_y1m(r).start()

    def d_stage(c, r):
        a = r % 5
        m_x2p(r).wait_recv()
        m_x2m(r).wait_recv()
        acc[a, :, seg_of(x), :CA] += x2r[r % DEPTH, 0].astype(F32) + x2r[r % DEPTH, 1].astype(F32)
        zs[r % DEPTH] = acc[a, :, seg_of(x), mate_a].astype(BF16)
        m_zred(r).start()

    def d2_stage(c, r):
        a = r % 5
        m_y1p(r).wait_recv()
        m_y1m(r).wait_recv()
        acc[a, :, seg_of(xp), own_b_left] += y1a[r % DEPTH].astype(F32)
        acc[a, :, seg_of(xm), own_b_right] += y1b[r % DEPTH].astype(F32)
        y2s[r % DEPTH, 0] = acc[a, :, seg_of(xp), own_b].astype(BF16)
        y2s[r % DEPTH, 1] = acc[a, :, seg_of(xm), own_b].astype(BF16)
        m_y2p(r).start()
        m_y2m(r).start()

    def finish_units(c, tot, cols):
        gate, up, dhid = tot[0], tot[1], tot[2]
        sig = jax.nn.sigmoid(gate)
        hh[c, 0, rows_of(x), cols] = (gate * sig * up).astype(BF16)
        hh[c, 1, rows_of(x), cols] = (dhid * up * sig * (1.0 + gate * (1.0 - sig))).astype(BF16)
        hh[c, 2, rows_of(x), cols] = (dhid * gate * sig).astype(BF16)

    def e_stage(c, r):
        a = r % 5
        for message in (m_x1p(r), m_x1m(r), m_x2p(r), m_x2m(r), m_zred(r)):
            message.wait_send()
        m_zred(r).wait_recv()
        finish_units(c, acc[a, :, seg_of(x), own_a] + zr[r % DEPTH].astype(F32), own_a)
        m_zgat(c, out_a).start()

    def e2_stage(c, r):
        a = r % 5
        for message in (m_y0(r), m_y1p(r), m_y1m(r), m_y2p(r), m_y2m(r)):
            message.wait_send()
        m_y2p(r).wait_recv()
        m_y2m(r).wait_recv()
        tot = acc[a, :, seg_of(x), own_b] + y2r[r % DEPTH, 0].astype(F32) + y2r[r % DEPTH, 1].astype(F32)
        finish_units(c, tot, own_b)
        m_k1p(c, x).start()
        m_k1m(c, x).start()

    def f_stage(c):
        m_zgat(c, in_a).wait_recv()
        m_g1p(c, x).start()
        m_g1m(c, x).start()

    def f2_stage(c):
        m_k1p(c, xm).wait_recv()
        m_k2p(c, xm).start()
        m_k1m(c, xp).wait_recv()
        m_k2m(c, xp).start()

    def g_stage(c):
        m_g1p(c, xm).wait_recv()
        m_g2p(c, xm).start()
        m_g1m(c, xp).wait_recv()
        m_g2m(c, xp).start()

    def g2_stage(c):
        m_k2p(c, xo).wait_recv()
        m_k2m(c, xo).wait_recv()
        m_k3(c, out_b).start()

    def h_stage(c):
        m_g2p(c, xo).wait_recv()
        m_g2m(c, xo).wait_recv()
        m_k3(c, in_b).wait_recv()
        m_cgat(c, q).start()

    def i_stage(c):
        m_cgat(c, 1 - q).wait_recv()
        for message in (
            m_zgat(c, out_a), m_g1p(c, x), m_g1m(c, x), m_g2p(c, xm), m_g2m(c, xp),
            m_cgat(c, q), m_k1p(c, x), m_k1m(c, x), m_k2p(c, xm), m_k2m(c, xp), m_k3(c, out_b),
        ):
            message.wait_send()
        part = jnp.dot(hh[c, 0], wd[...], preferred_element_type=F32)

        @pl.when(c == OWN)
        def _():
            mown[...] = part

        @pl.when(c == MATE)
        def _():
            mfar[...] = part

        @pl.when((c != OWN) & (c != MATE))
        def _():
            ms[c] = part.astype(BF16)
            m_mix(c).start()

        tokens_c = cols_of(c * ROWS, ROWS)
        hidt[:, tokens_c] = hh[c, 0].T
        tokt[:, tokens_c] = gat[c, :, :WIDTH].T

    def join_mixed():
        for c in (2, 3, 4):
            m_mix(c).wait_recv()
            mfar[...] += mr[c].astype(F32)
        m_far().start()

    def early_gradient(k):
        depth = EARLY * ROWS
        for n0, nw in DOT_COLUMNS:
            block = pl.ds(n0, nw)
            right = hh[:EARLY, k + 1, :, block].reshape(depth, nw)
            early[k, :, block] = jnp.dot(tokt[:, :depth], right, preferred_element_type=F32)

    plan = [
        (e_stage, 5, False), (c_stage, 2, False), (g2_stage, 9, True), (g_stage, 11, True),
        (f_stage, 9, True), (b_stage, 1, False), (d_stage, 3, False), (f2_stage, 7, True),
        (a_partials, 0, False), (h_stage, 12, True), (e2_stage, 4, False), (c2_stage, 2, False),
        (d2_stage, 3, False), (i_stage, 13, True),
    ]
    last = max(lag for _, lag, _ in plan)

    def step(i, carry):
        for stage, lag, back in plan:
            j = i - lag
            @pl.when((j >= 0) & (j < SLOTS))
            def _(stage=stage, j=j, back=back):
                if back:
                    stage(j)
                else:
                    slot = jnp.where(j == 0, OWN, jnp.where(j == 1, 0, jnp.where(j == 2, 5, j - 2)))
                    stage(jnp.where(j == 7, 6, slot), j)

        @pl.when(i == 1)
        def _():
            forward_tokens()

        @pl.when(i == 2)
        def _():
            send_far_tokens()

        @pl.when(i == JOIN)
        def _():
            join_mixed()

        for k, at in enumerate(EARLY_STEPS):

            @pl.when(i == at)
            def _(k=k):
                early_gradient(k)

        return carry

    lax.fori_loop(0, SLOTS + last, step, 0)

    for c in (0, 5, 6):
        m_mix(c).wait_recv()
        mown[...] += mr[c].astype(F32)
    m_far().wait_recv()
    mown[...] += mfr[...]

    def drain(c, carry):
        @pl.when((c != OWN) & (c != MATE))
        def _():
            m_mix(c).wait_send()

        @pl.when(c != OWN)
        def _():
            tok_msg(c, gat.at[OWN], core).wait_send()

        return carry

    lax.fori_loop(0, SLOTS, drain, 0)
    m_far().wait_send()


def exchange(ids, tokens, grad_out, wg, wu, wd):
    vmem = pl.BlockSpec(memory_space=pltpu.VMEM)
    hbm = pl.BlockSpec(memory_space=pltpu.HBM)
    total = SLOTS * ROWS
    kinds = len(NAMES)
    return pl.pallas_call(
        exchange_kernel,
        name="exchange",
        out_shape=(
            pltpu.VMEM((ROWS, WIDTH), F32),
            pltpu.VMEM((SLOTS, ROWS, 2 * WIDTH), BF16),
            pltpu.VMEM((WIDTH, total), BF16),
            pltpu.VMEM((UNITS, total), BF16),
            pltpu.VMEM((SLOTS, 3, ROWS, UNITS), BF16),
            pltpu.VMEM((len(EARLY_STEPS), WIDTH, UNITS), F32),
        ),
        in_specs=[hbm] * 6,
        out_specs=(vmem,) * 6,
        scratch_shapes=[
            pltpu.VMEM((SLOTS, ROWS), jnp.int32),
            pltpu.VMEM((ROWS, WIDTH), BF16),
            pltpu.VMEM((WIDTH, UNITS), BF16),
            pltpu.VMEM((WIDTH, UNITS), BF16),
            pltpu.VMEM((UNITS, WIDTH), BF16),
            pltpu.VMEM((5, 3, HALF, UNITS), F32),
            pltpu.VMEM((2, 3, HALF, UNITS), F32),
            pltpu.VMEM((2, 3, HALF, UNITS), F32),
            pltpu.VMEM((DEPTH, 3, SEG, CA), BF16),
            pltpu.VMEM((DEPTH, 3, SEG, OA), BF16),
            pltpu.VMEM((DEPTH, 3, SEG, KA), BF16),
            pltpu.VMEM((DEPTH, 2, 3, SEG, CA), BF16),
            pltpu.VMEM((DEPTH, 2, 3, SEG, CA), BF16),
            pltpu.VMEM((DEPTH, 3, SEG, OA), BF16),
            pltpu.VMEM((DEPTH, 3, SEG, OA), BF16),
            pltpu.VMEM((DEPTH, 3, HALF, OB), BF16),
            pltpu.VMEM((DEPTH, 3, HALF, OB), BF16),
            pltpu.VMEM((DEPTH, 3, SEG, OB), BF16),
            pltpu.VMEM((DEPTH, 3, SEG, OL), BF16),
            pltpu.VMEM((DEPTH, 3, SEG, OR), BF16),
            pltpu.VMEM((DEPTH, 2, 3, SEG, OB), BF16),
            pltpu.VMEM((DEPTH, 2, 3, SEG, OB), BF16),
            pltpu.VMEM((OWN, ROWS, WIDTH), BF16),
            pltpu.VMEM((OWN, ROWS, WIDTH), BF16),
            pltpu.VMEM((ROWS, WIDTH), F32),
            pltpu.VMEM((ROWS, WIDTH), F32),
            pltpu.SemaphoreType.DMA((kinds, SLOTS)),
            pltpu.SemaphoreType.DMA((kinds, SLOTS)),
            pltpu.SemaphoreType.DMA((SLOTS,)),
            pltpu.SemaphoreType.DMA((SLOTS,)),
            pltpu.SemaphoreType.DMA((3,)),
            pltpu.SemaphoreType.DMA((3,)),
        ],
        compiler_params=pltpu.CompilerParams(
            collective_id=0, has_side_effects=True, vmem_limit_bytes=30 * 2**20
        ),
        cost_estimate=pl.CostEstimate(
            flops=8 * total * WIDTH * UNITS, bytes_accessed=24 * 2**20, transcendentals=0
        ),
    )(ids, tokens, grad_out, wg, wu, wd)


GRAD_COLUMNS = 640


def grads_kernel(
    mown, gat, tokt, hidt, hh, early,
    mixed, grad_gate, grad_up, grad_down,
    mbuf, gbuf, ubuf, dbuf, sems, msem,
):
    mbuf[...] = mown[...].astype(BF16)
    mcopy = pltpu.make_async_copy(mbuf, mixed, msem)
    mcopy.start()
    total = SLOTS * ROWS
    sc = gat[:, :, WIDTH:].reshape(total, WIDTH)
    blocks = []
    for n in range(UNITS // GRAD_COLUMNS):
        cols = pl.ds(n * GRAD_COLUMNS, GRAD_COLUMNS)
        slot = n % 2
        copies = [
            pltpu.make_async_copy(gbuf.at[slot], grad_gate.at[:, cols], sems.at[0, slot]),
            pltpu.make_async_copy(ubuf.at[slot], grad_up.at[:, cols], sems.at[1, slot]),
            pltpu.make_async_copy(dbuf.at[slot], grad_down.at[cols, :], sems.at[2, slot]),
        ]
        blocks.append(copies)
        for k, buf in enumerate((gbuf, ubuf, dbuf)):
            if n >= 2:
                blocks[n - 2][k].wait()
            if k < 2:
                first = EARLY if k < len(EARLY_STEPS) else 0
                depth = total - first * ROWS
                right = hh[first:, k + 1, :, cols].reshape(depth, GRAD_COLUMNS)
                part = jnp.dot(tokt[:, first * ROWS :], right, preferred_element_type=F32)
                buf[slot] = part + early[k, :, cols] if first else part
            else:
                buf[slot] = jnp.dot(hidt[cols, :], sc, preferred_element_type=F32)
            copies[k].start()
    for copies in blocks[-2:]:
        for copy in copies:
            copy.wait()
    mcopy.wait()


def grads(*arrays):
    total = SLOTS * ROWS
    vmem = pl.BlockSpec(memory_space=pltpu.VMEM)
    hbm = pl.BlockSpec(memory_space=pl.ANY)
    return pl.pallas_call(
        grads_kernel,
        name="grads",
        out_shape=(
            jax.ShapeDtypeStruct((ROWS, WIDTH), BF16),
            jax.ShapeDtypeStruct((WIDTH, UNITS), F32),
            jax.ShapeDtypeStruct((WIDTH, UNITS), F32),
            jax.ShapeDtypeStruct((UNITS, WIDTH), F32),
        ),
        in_specs=[vmem] * 6,
        out_specs=(hbm,) * 4,
        scratch_shapes=[
            pltpu.VMEM((ROWS, WIDTH), BF16),
            pltpu.VMEM((2, WIDTH, GRAD_COLUMNS), F32),
            pltpu.VMEM((2, WIDTH, GRAD_COLUMNS), F32),
            pltpu.VMEM((2, GRAD_COLUMNS, WIDTH), F32),
            pltpu.SemaphoreType.DMA((3, 2)),
            pltpu.SemaphoreType.DMA,
        ],
        compiler_params=pltpu.CompilerParams(vmem_limit_bytes=9 * 2**20),
        cost_estimate=pl.CostEstimate(
            flops=6 * total * WIDTH * UNITS, bytes_accessed=12 * 2**20, transcendentals=0
        ),
    )(*arrays)


def shards(tokens, segment_ids, gate_weight, up_weight, down_weight, grad_out):
    ids = segment_ids.reshape(SLOTS, ROWS)
    arrays = (ids, tokens, grad_out, gate_weight, up_weight, down_weight)
    outs = exchange(*(pltpu.with_memory_space_constraint(a, pltpu.HBM) for a in arrays))
    return grads(*outs)


def solution(mesh):
    placed = (
        P("tensor", "dp"),
        P(),
        P("dp", "tensor"),
        P("dp", "tensor"),
        P("tensor", "dp"),
        P("tensor", "dp"),
    )
    return jax.shard_map(
        shards,
        mesh=mesh,
        in_specs=placed,
        out_specs=(P("tensor", "dp"), P("dp", "tensor"), P("dp", "tensor"), P("tensor", "dp")),
        check_vma=False,
    )
```
